32 devices in a mesh: section: 4 (over z), tensor: 4 (over y, x), dp: 2 (over core).
Axes of the slice: x: 2, y: 2, z: 4, core: 2. Of those that a mesh axis runs over, the one named last changes fastest.
Arguments:
- section_input: bfloat16 [4, 256, 4096], P('section', 'dp', 'tensor'), parts along dimension 1, may hold values from -6 to 6
- stash_pool: bfloat16 [4, 2, 256, 4096], P('section', None, 'dp', 'tensor'), parts along dimension 2, may hold values from -6 to 6
- reload_slot: int32 [4], P('section'), may hold values from 0 to 1
- cotangent: bfloat16 [4, 256, 4096], P('section', 'dp', 'tensor'), parts along dimension 1, may hold values from -6 to 6
- norm_gain: float32 [4, 4096], P('section', 'tensor'), may hold values from 0.5 to 6
- query_weight: bfloat16 [4, 4096, 4096], P('section', None, 'tensor'), may hold values from -0.09375 to 0.09375
- kv_weight: bfloat16 [4, 4096, 1024], P('section', 'tensor'), may hold values from -0.09375 to 0.09375
- out_weight: bfloat16 [4, 4096, 4096], P('section', 'tensor'), may hold values from -0.09375 to 0.09375
Outputs:
- next_input: bfloat16 [4, 256, 4096], P('section', 'dp', 'tensor'), parts along dimension 1
- received_stash: bfloat16 [4, 256, 4096], P('section', 'dp', 'tensor'), parts along dimension 1
- input_grad: bfloat16 [4, 256, 4096], P('section', 'dp', 'tensor'), parts along dimension 1
The draws below stay inside these ranges and needn't reach their ends.
There are 2 independent parts, one for each index of `dp`. The reference program is written for one: setup_inputs(seed, part) draws one part's arguments, and reference() takes and returns one part's arrays. A program takes and returns all parts, laid end to end along the dimension named above; an argument that names none is the same for every part. Nothing has to cross between parts.
All inputs are finite; a program needn't handle non-finite values.
Results may differ from the reference program's by a relative error of at most 0.024.
The reference program's roundings to bfloat16 on the way count: a program that leaves them out, or rounds other values in their place, can miss the bound.
Values may be sent and summed in bfloat16 or wider, within the bound.
A program may use at most 64 MiB of HBM per device.

```python
import jax
import jax.numpy as jnp
from jax import lax

D = 4096
HEADS = 32
KVH = 4
HD = 128
TOK = 128
SLOTS = 2
SECTIONS = 4


def draw_norm_gain(key, part):
    key = jax.random.fold_in(key, 11)
    return jnp.clip(1.0 + 0.1 * jax.random.normal(key, (SECTIONS, D), jnp.float32), 0.5, 1.5)


def set_ends(entries, stream_key, least, top_value):
    longest = entries.shape.index(max(entries.shape))
    spots = []
    for shift in (0, 1):
        where = [jax.random.randint(jax.random.fold_in(stream_key, axis), (), 0, length) for axis, length in enumerate(entries.shape)]
        where[longest] = (where[longest] + shift) % entries.shape[longest]
        spots.append(tuple(where))
    return entries.at[spots[0]].set(least).at[spots[1]].set(top_value)


def shard_levels(stream_key, extent, split, least, top_value):
    factor_of = 1.0
    for position, parts in split:
        heights = jax.random.uniform(jax.random.fold_in(jax.random.fold_in(stream_key, 6), position), (parts,), jnp.float32, least / len(split), top_value / len(split))
        factor_of = factor_of * jnp.repeat(jnp.exp(heights), extent[position] // parts).reshape((-1,) + (1,) * (len(extent) - 1 - position))
    return factor_of


def centred(rng, dims, width, reach, split=(), kind=jnp.bfloat16):
    entries = width * jax.random.normal(rng, dims, jnp.float32)
    if split:
        entries = entries * shard_levels(rng, dims, split, -0.22, 0.18)
    return jnp.clip(entries, -reach, reach).astype(kind)


def setup_inputs(seed: int = 0, part: int = 0) -> dict:
    key_list = jax.random.split(jax.random.key(seed), 9)
    own_keys = jax.random.split(jax.random.fold_in(key_list[8], part), 9)
    return {
        "section_input": centred(own_keys[0], (SECTIONS, TOK, D), 1.0, 6.0, ((0, 4), (2, 4))),
        "stash_pool": centred(own_keys[1], (SECTIONS, SLOTS, TOK, D), 1.0, 6.0, ((0, 4), (3, 4))),
        "reload_slot": set_ends(jax.random.randint(key_list[2], (SECTIONS,), 0, SLOTS), jax.random.fold_in(key_list[2], 1), 0, SLOTS - 1).astype(jnp.int32),
        "cotangent": centred(own_keys[3], (SECTIONS, TOK, D), 1.0, 6.0, ((0, 4), (2, 4))),
        "norm_gain": draw_norm_gain(jax.random.fold_in(key_list[8], 71), part),
        "query_weight": centred(key_list[5], (SECTIONS, D, HEADS * HD), D ** -0.5, 0.09375, ((0, 4), (2, 4))),
        "kv_weight": centred(key_list[6], (SECTIONS, D, 2 * KVH * HD), D ** -0.5, 0.09375, ((0, 4), (1, 4))),
        "out_weight": centred(key_list[7], (SECTIONS, HEADS * HD, D), (HEADS * HD) ** -0.5, 0.09375, ((0, 4), (1, 4))),
    }


norm_eps = 1e-05

def rope_tables(row_total, head_width):
    half_width = head_width // 2
    inverse = 10000.0 ** (-2.0 * jnp.arange(half_width, dtype=jnp.float32) / head_width)
    angles = jnp.arange(row_total, dtype=jnp.float32)[:, None] * inverse[None, :]
    return (jnp.cos(angles)[:, None, :], jnp.sin(angles)[:, None, :])

def rotate(values, cos_table, sin_table):
    half_width = values.shape[-1] // 2
    first_half = values[..., :half_width]
    second_half = values[..., half_width:]
    return jnp.concatenate([first_half * cos_table - second_half * sin_table, second_half * cos_table + first_half * sin_table], axis=-1)

def unrotate(values, cos_table, sin_table):
    half_width = values.shape[-1] // 2
    first_half = values[..., :half_width]
    second_half = values[..., half_width:]
    return jnp.concatenate([first_half * cos_table + second_half * sin_table, second_half * cos_table - first_half * sin_table], axis=-1)

def normalize(token_rows, gain_row):
    rows_wide = token_rows.astype(jnp.float32)
    factor = lax.rsqrt(lax.optimization_barrier(jnp.mean(rows_wide * rows_wide, axis=-1, keepdims=True)) + norm_eps)
    return rows_wide * factor * gain_row

def heads_forward(normed, query_w, kv_w, cos_table, sin_table):
    tokens_here = normed.shape[0]
    kv_all = jnp.dot(normed, kv_w, preferred_element_type=jnp.float32).reshape(tokens_here, 2, KVH, HD)
    key_heads = rotate(kv_all[:, 0], cos_table, sin_table).astype(jnp.bfloat16)
    value_heads = kv_all[:, 1].astype(jnp.bfloat16)
    query_heads = jnp.dot(normed, query_w, preferred_element_type=jnp.float32).reshape(tokens_here, HEADS, HD)
    query_heads = (rotate(query_heads, cos_table, sin_table) * HD ** (-0.5)).astype(jnp.bfloat16)
    grouped = query_heads.reshape(tokens_here, KVH, HEADS // KVH, HD)
    scores = jnp.einsum('tkgd,skd->kgts', grouped.astype(jnp.float32), key_heads.astype(jnp.float32))
    causal = jnp.arange(tokens_here)[:, None] >= jnp.arange(tokens_here)[None, :]
    scores = jnp.where(causal, scores, -1e+30)
    shifted = jnp.exp(scores - lax.optimization_barrier(jnp.max(scores, axis=-1, keepdims=True)))
    softmax_probs = shifted / lax.optimization_barrier(jnp.sum(shifted, axis=-1, keepdims=True))
    prob_weights = softmax_probs.astype(jnp.bfloat16)
    attended = jnp.einsum('kgts,skd->tkgd', prob_weights.astype(jnp.float32), value_heads.astype(jnp.float32))
    attended = attended.astype(jnp.bfloat16).reshape(tokens_here, HEADS * HD)
    return (grouped, key_heads, value_heads, softmax_probs, prob_weights, attended)

def section_forward(token_rows, gain_row, query_w, kv_w, out_w, cos_table, sin_table):
    normed = normalize(token_rows, gain_row).astype(jnp.bfloat16)
    attended = heads_forward(normed, query_w, kv_w, cos_table, sin_table)[5]
    projected = jnp.dot(attended, out_w, preferred_element_type=jnp.float32)
    return (token_rows.astype(jnp.float32) + projected).astype(jnp.bfloat16)

def section_backward(back_rows, cot_rows, gain_row, query_w, kv_w, out_w, cos_table, sin_table):
    tokens_here = back_rows.shape[0]
    normed = normalize(back_rows, gain_row).astype(jnp.bfloat16)
    grouped, key_heads, value_heads, softmax_probs, prob_weights, _ = heads_forward(normed, query_w, kv_w, cos_table, sin_table)
    grad_out = jnp.dot(cot_rows, out_w.T, preferred_element_type=jnp.float32).astype(jnp.bfloat16)
    grad_out = grad_out.reshape(tokens_here, KVH, HEADS // KVH, HD).astype(jnp.float32)
    grad_probs = jnp.einsum('tkgd,skd->kgts', grad_out, value_heads.astype(jnp.float32))
    row_delta = lax.optimization_barrier(jnp.sum(softmax_probs * grad_probs, axis=-1, keepdims=True))
    grad_scores = (softmax_probs * (grad_probs - row_delta)).astype(jnp.bfloat16).astype(jnp.float32)
    grad_query = jnp.einsum('kgts,skd->tkgd', grad_scores, key_heads.astype(jnp.float32)).reshape(tokens_here, HEADS, HD)
    grad_query = (unrotate(grad_query, cos_table, sin_table) * HD ** (-0.5)).astype(jnp.bfloat16).reshape(tokens_here, HEADS * HD)
    grad_key = jnp.einsum('kgts,tkgd->skd', grad_scores, grouped.astype(jnp.float32))
    grad_key = unrotate(grad_key, cos_table, sin_table)
    grad_value = jnp.einsum('kgts,tkgd->skd', prob_weights.astype(jnp.float32), grad_out)
    grad_kv = jnp.stack([grad_key, grad_value], axis=1).reshape(tokens_here, 2 * KVH * HD).astype(jnp.bfloat16)
    grad_normed = jnp.dot(grad_query, query_w.T, preferred_element_type=jnp.float32) + jnp.dot(grad_kv, kv_w.T, preferred_element_type=jnp.float32)
    rows_wide = back_rows.astype(jnp.float32)
    factor = lax.rsqrt(lax.optimization_barrier(jnp.mean(rows_wide * rows_wide, axis=-1, keepdims=True)) + norm_eps)
    scaled = grad_normed * gain_row
    grad_rows = factor * scaled - rows_wide * factor * factor * factor * lax.optimization_barrier(jnp.mean(scaled * rows_wide, axis=-1, keepdims=True))
    return (cot_rows.astype(jnp.float32) + grad_rows).astype(jnp.bfloat16)

def reference(section_input, stash_pool, reload_slot, cotangent, norm_gain, query_weight, kv_weight, out_weight):
    cos_table, sin_table = rope_tables(TOK, HD)
    section_ids = jnp.arange(SECTIONS, dtype=jnp.int32)
    is_early = (section_ids < SECTIONS // 2)[:, None, None]
    picked = stash_pool[section_ids, reload_slot.astype(jnp.int32)]
    sending = jnp.where(is_early, section_input, picked)
    received = sending[::-1]
    back_input = jnp.where(is_early, received, section_input)

    def per_section(pieces):
        token_rows, back_rows, cot_rows, gain_row, query_w, kv_w, out_w = pieces
        layer_out = section_forward(token_rows, gain_row, query_w, kv_w, out_w, cos_table, sin_table)
        grad_local = section_backward(back_rows, cot_rows, gain_row, query_w, kv_w, out_w, cos_table, sin_table)
        return (layer_out, grad_local)
    layer_outputs, layer_grads = lax.map(per_section, (section_input, back_input, cotangent, norm_gain, query_weight, kv_weight, out_weight))
    zero_block = jnp.zeros_like(layer_outputs[:1])
    next_input = jnp.concatenate([zero_block, layer_outputs[:-1]], axis=0)
    input_grad = jnp.concatenate([layer_grads[1:], zero_block], axis=0)
    return (next_input, received, input_grad)
```

```python
import functools

import jax
import jax.numpy as jnp
import numpy as np
from jax import lax
from jax.experimental import pallas as pl
from jax.experimental.pallas import tpu as pltpu
from jax.sharding import PartitionSpec as P

HEADS = 32
KVH = 4
HD = 128
PAIR = 2
TILE = 256
SUMROWS = 8
ZCHUNKS = 4

norm_eps = 1e-05
f32 = jnp.float32
bf16 = jnp.bfloat16


def rope_constants(tokens):
    half = HD // 2
    inverse = np.float32(10000.0) ** (
        np.float32(-2.0) * np.arange(half, dtype=np.float32) / np.float32(HD)
    )
    angles = np.arange(tokens, dtype=np.float32)[:, None] * inverse[None, :].astype(np.float32)
    cos, sin = np.cos(angles), np.sin(angles)
    return (
        np.concatenate([cos, cos], axis=1).astype(np.float32),
        np.concatenate([-sin, sin], axis=1).astype(np.float32),
    )


def flipped(index, bits):
    place = 1
    while place <= bits:
        if bits & place:
            bit = lax.rem(lax.div(index, place), 2)
            index = index + place * (1 - 2 * bit)
        place *= 2
    return index


def dot_nn(a, b):
    return jnp.dot(a, b, preferred_element_type=f32)


def dot_nt(a, b):
    return lax.dot_general(a, b, (((1,), (1,)), ((), ())), preferred_element_type=f32)


def dot_tn(a, b):
    return lax.dot_general(a, b, (((0,), (0,)), ((), ())), preferred_element_type=f32)


def layer_kernel(
    ways,
    sections,
    slot_ref,
    x_ref,
    stash_ref,
    cot_ref,
    gain_ref,
    cos_ref,
    sin_ref,
    qw_hbm,
    kvw_hbm,
    ow_hbm,
    next_ref,
    travel_ref,
    igrad_ref,
    qw,
    kvw,
    ow,
    xg,
    bg,
    cg,
    gg,
    fn,
    bn,
    fact,
    qf,
    qb,
    go,
    att,
    gqb,
    kvf_p,
    kvf_r,
    kvb_p,
    kvb_r,
    out_p,
    out_s,
    out_r,
    gq_p,
    gq_s,
    gq_r,
    gk_s,
    gk_r,
    gk_acc,
    gk_full,
    trav,
    lo,
    gl,
    scaled,
    msum,
    wsem,
    ssem,
    rsem,
):
    tokens, width = x_ref.shape
    heads_here = qw.shape[1] // HD
    model = width * ways
    half = tokens // 2
    upper, lower = pl.ds(0, half), pl.ds(half, half)
    me = lax.axis_index("tensor")
    sec = lax.axis_index("section")
    early = sec < sections // 2
    has_prev = sec > 0
    has_next = sec < sections - 1
    mirror = sections - 1 - sec
    prev = jnp.maximum(sec - 1, 0)
    nxt = jnp.minimum(sec + 1, sections - 1)
    peers = [flipped(me, k) for k in range(ways)]
    rows_of = [pl.ds(pl.multiple_of(p * width, width), width) for p in peers]
    relay = ways == 4
    per_group = ways // KVH
    groups = [lax.div(p, per_group) for p in peers]

    loads = [
        pltpu.make_async_copy(a, b, wsem.at[i])
        for i, (a, b) in enumerate(((kvw_hbm, kvw), (qw_hbm, qw), (ow_hbm, ow)))
    ]
    for load in loads:
        load.start()

    used = []
    pending = []

    def send(src, dst, axis, peer, start=True):
        i = len(used)
        used.append(i)
        copy = pltpu.make_async_remote_copy(
            src_ref=src,
            dst_ref=dst,
            send_sem=ssem.at[i],
            recv_sem=rsem.at[i],
            device_id={axis: peer},
            device_id_type=pl.DeviceIdType.MESH,
        )
        if start:
            copy.start()
            pending.append(copy)
        return copy

    def to_peer(k, src, dst):
        return send(src, dst, "tensor", peers[k])

    barrier = pltpu.get_barrier_semaphore()

    def greet(axis, peer):
        pl.semaphore_signal(
            barrier, inc=1, device_id={axis: peer}, device_id_type=pl.DeviceIdType.MESH
        )

    for k in range(1, ways):
        greet("tensor", peers[k])
    greet("section", mirror)

    @pl.when(has_prev)
    def _():
        greet("section", prev)

    @pl.when(has_next)
    def _():
        greet("section", nxt)

    @pl.when(early)
    def _():
        trav[...] = x_ref[...]

    @pl.when(jnp.logical_not(early))
    def _():
        trav[...] = stash_ref[slot_ref[0]]

    xg[0] = x_ref[...]
    cg[0] = cot_ref[...]
    gg[0] = jnp.broadcast_to(gain_ref[...], gg.shape[1:])

    pl.semaphore_wait(barrier, ways + jnp.minimum(sec, 1) + jnp.minimum(sections - 1 - sec, 1))

    def gather_start(buf):
        if relay:
            return [to_peer(k, buf.at[0], buf.at[k]) for k in (1, 2)]
        return [to_peer(k, buf.at[0], buf.at[k]) for k in range(1, ways)]

    def gather_pass_on(buf, copies):
        if not relay:
            return copies
        copies[0].wait_recv()
        first = to_peer(2, buf.at[1, upper], buf.at[3, upper])
        copies[1].wait_recv()
        second = to_peer(1, buf.at[2, lower], buf.at[3, lower])
        return [first, second]

    def finish(copies):
        for copy in copies:
            copy.wait_recv()

    order = (3, 1, 2, 0) if relay else tuple(range(1, ways)) + (0,)

    def reduce_send(k, stage, land):
        if k == 0:
            return []
        if not relay:
            return [to_peer(k, stage.at[k], land.at[k])]
        if k == 3:
            return [
                to_peer(1, stage.at[3, upper], land.at[2, upper]),
                to_peer(2, stage.at[3, lower], land.at[1, lower]),
            ]
        if k == 1:
            return [to_peer(1, stage.at[1, upper], land.at[0, upper])]
        return [to_peer(2, stage.at[2, lower], land.at[0, lower])]

    def reduce_pass_on(copies, part, stage, land):
        if not relay:
            return copies
        copies[0].wait_recv()
        stage[2, upper] = (part[2, upper] + land[2, upper].astype(f32)).astype(stage.dtype)
        first = to_peer(2, stage.at[2, upper], land.at[3, upper])
        copies[1].wait_recv()
        stage[1, lower] = (part[1, lower] + land[1, lower].astype(f32)).astype(stage.dtype)
        second = to_peer(1, stage.at[1, lower], land.at[3, lower])
        return copies[2:] + [first, second]

    def reduced(part, land, rows, cols):
        total = part[0, rows, cols]
        for k in (0, 3) if relay else range(1, ways):
            total = total + land[k, rows, cols].astype(f32)
        return total

    def normalize(raw, out, keep):
        step = 16

        def body(i, carry):
            rows = pl.ds(pl.multiple_of(i * step, step), step)
            total = jnp.zeros((step, 1), f32)
            for k in range(ways):
                v = raw[k, rows, :].astype(f32)
                total = total + jnp.sum(v * v, axis=-1, keepdims=True)
            factor = lax.rsqrt(total / model + norm_eps)
            for k in range(ways):
                v = raw[k, rows, :].astype(f32)
                out[k, rows, :] = (v * factor * gg[k, 0:1, :]).astype(bf16)
            if keep:
                fact[rows, :] = jnp.broadcast_to(factor, (step, HD))
            return carry

        lax.fori_loop(0, tokens // step, body, 0)

    def kv_terms(normed, part, land):
        copies = []
        for k in order:
            key_cols = pl.ds(pl.multiple_of(groups[k] * HD, HD), HD)
            value_cols = pl.ds(pl.multiple_of((KVH + groups[k]) * HD, HD), HD)
            part[k, :, 0:HD] = dot_nn(normed[0], kvw[:, key_cols])
            part[k, :, HD : 2 * HD] = dot_nn(normed[0], kvw[:, value_cols])
            copies += reduce_send(k, part, land)
        return copies

    def rotate(u):
        return u * cos_ref[...] + pltpu.roll(u, HD // 2, 1) * sin_ref[...]

    def unrotate(u):
        return u * cos_ref[...] - pltpu.roll(u, HD // 2, 1) * sin_ref[...]

    per_tile = TILE // HD
    scale = HD ** (-0.5)

    def queries(normed, out):
        def body(n, carry):
            cols = pl.ds(pl.multiple_of(n * TILE, TILE), TILE)
            acc = dot_nn(normed[0], qw[rows_of[0], cols])
            for k in range(1, ways):
                acc = acc + dot_nn(normed[k], qw[rows_of[k], cols])
            for j in range(per_tile):
                head = acc[:, j * HD : (j + 1) * HD]
                out[n * per_tile + j] = (rotate(head) * scale).astype(bf16)
            return carry

        lax.fori_loop(0, heads_here // per_tile, body, 0)

    def key_value(part, land):
        everything = pl.ds(0, tokens)
        key = rotate(reduced(part, land, everything, pl.ds(0, HD))).astype(bf16)
        value = reduced(part, land, everything, pl.ds(HD, HD)).astype(bf16)
        return key, value

    span = PAIR * tokens
    position = lax.rem(lax.broadcasted_iota(jnp.int32, (span, tokens), 0), tokens)
    seen = position >= lax.broadcasted_iota(jnp.int32, (span, tokens), 1)

    def probabilities(q, key):
        scores = jnp.where(seen, dot_nt(q, key), -1e30)
        shifted = jnp.exp(scores - jnp.max(scores, axis=-1, keepdims=True))
        return shifted * (1.0 / jnp.sum(shifted, axis=-1, keepdims=True))

    def project(source, weight_tile, part, stage, land):
        copies = []
        for k in order:

            def body(n, carry, k=k):
                cols = pl.ds(pl.multiple_of(n * TILE, TILE), TILE)
                value = weight_tile(source, k, n)
                if not (relay and k == 3):
                    part[k, :, cols] = value
                if k:
                    stage[k, :, cols] = value.astype(bf16)
                return carry

            lax.fori_loop(0, width // TILE, body, 0)
            copies += reduce_send(k, stage, land)
        return copies

    def out_tile(source, k, n):
        cols = pl.ds(pl.multiple_of(peers[k] * width + n * TILE, TILE), TILE)
        return dot_nn(source[...], ow[:, cols])

    def query_tile(source, k, n):
        rows = pl.ds(pl.multiple_of(peers[k] * width + n * TILE, TILE), TILE)
        return dot_nt(source[...], qw[rows, :])

    travel_copy = send(trav, travel_ref, "section", mirror)
    gain_copies = [to_peer(k, gg.at[0], gg.at[k]) for k in range(1, ways)]
    x_copies = gather_start(xg)
    x_copies = gather_pass_on(xg, x_copies)

    travel_copy.wait_recv()

    @pl.when(early)
    def _():
        bg[0] = travel_ref[...]

    @pl.when(jnp.logical_not(early))
    def _():
        bg[0] = x_ref[...]

    b_copies = gather_start(bg)
    finish(gain_copies)
    finish(x_copies)
    normalize(xg, fn, False)
    loads[0].wait()
    kvf = kv_terms(fn, kvf_p, kvf_r)
    loads[1].wait()
    queries(fn, qf)
    kvf = reduce_pass_on(kvf, kvf_p, kvf_p, kvf_r)
    b_copies = gather_pass_on(bg, b_copies)
    c_copies = gather_start(cg)
    finish(kvf)
    key, value = key_value(kvf_p, kvf_r)
    for i in range(heads_here // PAIR):
        q = qf[PAIR * i : PAIR * (i + 1)].reshape(span, HD)
        weights = probabilities(q, key).astype(bf16)
        result = dot_nn(weights, value).astype(bf16)
        for j in range(PAIR):
            head = PAIR * i + j
            att[:, head * HD : (head + 1) * HD] = result[j * tokens : (j + 1) * tokens]

    finish(b_copies)
    normalize(bg, bn, True)
    kvb = kv_terms(bn, kvb_p, kvb_r)
    loads[2].wait()
    outs = project(att, out_tile, out_p, out_s, out_r)
    queries(bn, qb)
    kvb = reduce_pass_on(kvb, kvb_p, kvb_p, kvb_r)
    c_copies = gather_pass_on(cg, c_copies)
    outs = reduce_pass_on(outs, out_p, out_s, out_r)
    finish(c_copies)

    def cot_body(n, carry):
        rows = pl.ds(pl.multiple_of(n * TILE, TILE), TILE)
        acc = dot_nt(cg[0], ow[rows, rows_of[0]])
        for k in range(1, ways):
            acc = acc + dot_nt(cg[k], ow[rows, rows_of[k]])
        for j in range(per_tile):
            go[n * per_tile + j] = acc[:, j * HD : (j + 1) * HD].astype(bf16)
        return carry

    lax.fori_loop(0, heads_here // per_tile, cot_body, 0)
    finish(kvb)
    key, value = key_value(kvb_p, kvb_r)
    grad_key = jnp.zeros((tokens, HD), f32)
    grad_value = jnp.zeros((tokens, HD), f32)
    for i in range(heads_here // PAIR):
        q = qb[PAIR * i : PAIR * (i + 1)].reshape(span, HD)
        g = go[PAIR * i : PAIR * (i + 1)].reshape(span, HD)
        probs = probabilities(q, key)
        grad_probs = dot_nt(g, value)
        delta = jnp.sum(probs * grad_probs, axis=-1, keepdims=True)
        grad_scores = (probs * (grad_probs - delta)).astype(bf16)
        grad_q = dot_nn(grad_scores, key)
        for j in range(PAIR):
            head = PAIR * i + j
            turned = unrotate(grad_q[j * tokens : (j + 1) * tokens]) * scale
            gqb[:, head * HD : (head + 1) * HD] = turned.astype(bf16)
        grad_key = grad_key + dot_tn(grad_scores, q)
        grad_value = grad_value + dot_tn(probs.astype(bf16), g)
    gk_r[0, :, 0:HD] = unrotate(grad_key).astype(gk_r.dtype)
    gk_r[0, :, HD : 2 * HD] = grad_value.astype(gk_r.dtype)
    gk_copies = [to_peer(k, gk_r.at[0], gk_r.at[k]) for k in range(1, ways)]
    grads = project(gqb, query_tile, gq_p, gq_s, gq_r)

    finish(outs)
    chunk = tokens // ZCHUNKS
    next_copies = []
    for c in range(ZCHUNKS):
        rows = pl.ds(c * chunk, chunk)
        total = reduced(out_p, out_r, rows, pl.ds(0, width))
        lo[rows, :] = (x_ref[rows, :].astype(f32) + total).astype(bf16)
        copy = send(lo.at[rows], next_ref.at[rows], "section", nxt, start=False)
        pl.when(has_next)(copy.start)
        next_copies.append(copy)

    grads = reduce_pass_on(grads, gq_p, gq_s, gq_r)

    finish(gk_copies)
    if per_group == 1:
        for k in range(ways):
            key_cols = pl.ds(pl.multiple_of(groups[k] * HD, HD), HD)
            value_cols = pl.ds(pl.multiple_of((KVH + groups[k]) * HD, HD), HD)
            gk_full[:, key_cols] = gk_r[k, :, 0:HD]
            gk_full[:, value_cols] = gk_r[k, :, HD : 2 * HD]
    else:
        gk_acc[...] = jnp.zeros_like(gk_acc)
        for k in range(ways):
            key_cols = pl.ds(pl.multiple_of(groups[k] * HD, HD), HD)
            value_cols = pl.ds(pl.multiple_of((KVH + groups[k]) * HD, HD), HD)
            gk_acc[:, key_cols] += gk_r[k, :, 0:HD].astype(f32)
            gk_acc[:, value_cols] += gk_r[k, :, HD : 2 * HD].astype(f32)
        gk_full[...] = gk_acc[...].astype(bf16)
    for n in range(width // TILE):
        cols = pl.ds(n * TILE, TILE)
        gq_p[0, :, cols] += dot_nt(gk_full[...], kvw[cols, :])

    finish(grads)
    row_sum = jnp.zeros((tokens, 1), f32)
    for n in range(width // TILE):
        cols = pl.ds(n * TILE, TILE)
        part = reduced(gq_p, gq_r, pl.ds(0, tokens), cols) * gain_ref[:, cols]
        scaled[:, cols] = part
        row_sum = row_sum + jnp.sum(part * bg[0, :, cols].astype(f32), axis=-1, keepdims=True)
    eye = lax.broadcasted_iota(jnp.int32, (tokens, tokens), 0) == lax.broadcasted_iota(
        jnp.int32, (tokens, tokens), 1
    )
    as_row = jnp.sum(jnp.where(eye, row_sum, 0.0), axis=0, keepdims=True)
    msum[0] = jnp.broadcast_to(as_row, (SUMROWS, tokens))
    finish([to_peer(k, msum.at[0], msum.at[k]) for k in range(1, ways)])
    total = msum[0, 0:1, :]
    for k in range(1, ways):
        total = total + msum[k, 0:1, :]
    mean = jnp.sum(jnp.where(eye, total, 0.0), axis=1, keepdims=True) / model
    grad_copies = []
    for c in range(ZCHUNKS):
        rows = pl.ds(c * chunk, chunk)
        factor = fact[rows, 0:1]
        back = bg[0, rows, :].astype(f32)
        cube = factor * factor * factor * mean[c * chunk : (c + 1) * chunk]
        grad_rows = factor * scaled[rows, :] - back * cube
        gl[rows, :] = (cot_ref[rows, :].astype(f32) + grad_rows).astype(bf16)
        copy = send(gl.at[rows], igrad_ref.at[rows], "section", prev, start=False)
        pl.when(has_prev)(copy.start)
        grad_copies.append(copy)

    @pl.when(jnp.logical_not(has_prev))
    def _():
        next_ref[...] = jnp.zeros_like(next_ref)

    @pl.when(jnp.logical_not(has_next))
    def _():
        igrad_ref[...] = jnp.zeros_like(igrad_ref)

    for copy in pending:
        copy.wait_send()

    @pl.when(has_next)
    def _():
        for copy in next_copies:
            copy.wait_send()
        for copy in grad_copies:
            copy.wait_recv()

    @pl.when(has_prev)
    def _():
        for copy in next_copies:
            copy.wait_recv()
        for copy in grad_copies:
            copy.wait_send()


def copies_needed(ways):
    if ways == 4:
        return 1 + 3 + 3 * 4 + 4 * 6 + 3 + 3 + 2 * ZCHUNKS
    return 1 + (ways - 1) * 10 + 2 * ZCHUNKS


def per_device(
    ways,
    sections,
    section_input,
    stash_pool,
    reload_slot,
    cotangent,
    norm_gain,
    query_weight,
    kv_weight,
    out_weight,
):
    _, tokens, width = section_input.shape
    model = width * ways
    local = query_weight.shape[2]
    heads_here = local // HD
    cos_table, sin_table = rope_constants(tokens)
    grad_kv_type = bf16 if ways == KVH else f32
    copies = copies_needed(ways)
    vmem = pl.BlockSpec(memory_space=pltpu.VMEM)
    block = jax.ShapeDtypeStruct((tokens, width), bf16)
    gathered = pltpu.VMEM((ways, tokens, width), bf16)
    wide = pltpu.VMEM((ways, tokens, width), f32)
    kv_block = pltpu.VMEM((ways, tokens, 2 * HD), f32)
    head_block = pltpu.VMEM((heads_here, tokens, HD), bf16)
    flat = pltpu.VMEM((tokens, local), bf16)
    scratch = [
        pltpu.VMEM((model, local), bf16),
        pltpu.VMEM((width, 2 * KVH * HD), bf16),
        pltpu.VMEM((local, model), bf16),
        gathered,
        gathered,
        gathered,
        pltpu.VMEM((ways, SUMROWS, width), f32),
        gathered,
        gathered,
        pltpu.VMEM((tokens, HD), f32),
        head_block,
        head_block,
        head_block,
        flat,
        flat,
        kv_block,
        kv_block,
        kv_block,
        kv_block,
        wide,
        gathered,
        gathered,
        wide,
        gathered,
        gathered,
        pltpu.VMEM((tokens, 2 * HD), grad_kv_type),
        pltpu.VMEM((ways, tokens, 2 * HD), grad_kv_type),
        pltpu.VMEM((tokens, 2 * KVH * HD), f32),
        pltpu.VMEM((tokens, 2 * KVH * HD), bf16),
        pltpu.VMEM((tokens, width), bf16),
        pltpu.VMEM((tokens, width), bf16),
        pltpu.VMEM((tokens, width), bf16),
        pltpu.VMEM((tokens, width), f32),
        pltpu.VMEM((ways, SUMROWS, tokens), f32),
        pltpu.SemaphoreType.DMA((3,)),
        pltpu.SemaphoreType.DMA((copies,)),
        pltpu.SemaphoreType.DMA((copies,)),
    ]
    macs = 5 * tokens * model * local + 3 * tokens * width * 2 * KVH * HD
    next_input, received, input_grad = pl.pallas_call(
        functools.partial(layer_kernel, ways, sections),
        out_shape=(block, block, block),
        in_specs=[pl.BlockSpec(memory_space=pltpu.SMEM)]
        + [vmem] * 6
        + [pl.BlockSpec(memory_space=pl.ANY)] * 3,
        out_specs=(vmem, vmem, vmem),
        scratch_shapes=scratch,
        cost_estimate=pl.CostEstimate(
            flops=2 * macs,
            bytes_accessed=2 * (2 * model * local + width * 2 * KVH * HD + 8 * tokens * width),
            transcendentals=2 * heads_here * tokens * tokens,
        ),
        compiler_params=pltpu.CompilerParams(
            collective_id=0, has_side_effects=True, vmem_limit_bytes=56 * 1024 * 1024
        ),
        name="attention_layer",
    )(
        reload_slot,
        section_input[0],
        stash_pool[0],
        cotangent[0],
        norm_gain,
        jnp.asarray(cos_table),
        jnp.asarray(sin_table),
        query_weight[0],
        kv_weight[0],
        out_weight[0],
    )
    return (next_input[None], received[None], input_grad[None])


def solution(mesh):
    return jax.shard_map(
        functools.partial(per_device, mesh.shape["tensor"], mesh.shape["section"]),
        mesh=mesh,
        in_specs=(
            P("section", "dp", "tensor"),
            P("section", None, "dp", "tensor"),
            P("section"),
            P("section", "dp", "tensor"),
            P("section", "tensor"),
            P("section", None, "tensor"),
            P("section", "tensor", None),
            P("section", "tensor", None),
        ),
        out_specs=(
            P("section", "dp", "tensor"),
            P("section", "dp", "tensor"),
            P("section", "dp", "tensor"),
        ),
        check_vma=False,
    )
```

```python
import functools

import jax
import jax.numpy as jnp
import numpy as np
from jax import lax
from jax.experimental import pallas as pl
from jax.experimental.pallas import tpu as pltpu
from jax.sharding import PartitionSpec as P

HEADS = 32
KVH = 4
HD = 128
PAIR = 2
TILE = 256
SUMROWS = 8
PIECES = 2

norm_eps = 1e-05
f32 = jnp.float32
bf16 = jnp.bfloat16


def rope_constants(tokens):
    half = HD // 2
    inverse = np.float32(10000.0) ** (
        np.float32(-2.0) * np.arange(half, dtype=np.float32) / np.float32(HD)
    )
    angles = np.arange(tokens, dtype=np.float32)[:, None] * inverse[None, :].astype(np.float32)
    cos, sin = np.cos(angles), np.sin(angles)
    return (
        np.concatenate([cos, cos], axis=1).astype(np.float32),
        np.concatenate([-sin, sin], axis=1).astype(np.float32),
    )


def flipped(index, bits):
    place = 1
    while place <= bits:
        if bits & place:
            bit = lax.rem(lax.div(index, place), 2)
            index = index + place * (1 - 2 * bit)
        place *= 2
    return index


def dot_nn(a, b):
    return jnp.dot(a, b, preferred_element_type=f32)


def dot_nt(a, b):
    return lax.dot_general(a, b, (((1,), (1,)), ((), ())), preferred_element_type=f32)


def dot_tn(a, b):
    return lax.dot_general(a, b, (((0,), (0,)), ((), ())), preferred_element_type=f32)


def layer_kernel(
    ways,
    sections,
    slot_ref,
    x_ref,
    stash_ref,
    cot_ref,
    gain_ref,
    cos_ref,
    sin_ref,
    qw_hbm,
    kvw_hbm,
    ow_hbm,
    next_ref,
    travel_ref,
    igrad_ref,
    qw,
    kvw,
    ow,
    cg,
    fn,
    bn,
    back,
    c_acc,
    f_acc,
    b_acc,
    qf,
    qb,
    go,
    att,
    gqb,
    kvf_p,
    kvf_r,
    kvb_p,
    kvb_r,
    out_p,
    out_s,
    out_r,
    gq_p,
    gq_s,
    gq_r,
    gk_r,
    gk_acc,
    gk_full,
    trav,
    lo,
    gl,
    f_sum,
    b_sum,
    m_sum,
    wsem,
    ssem,
    rsem,
):
    tokens, width = x_ref.shape
    heads_here = qw.shape[1] // HD
    model = width * ways
    half = tokens // 2
    upper, lower = pl.ds(0, half), pl.ds(half, half)
    me = lax.axis_index("tensor")
    sec = lax.axis_index("section")
    early = sec < sections // 2
    has_prev = sec > 0
    has_next = sec < sections - 1
    mirror = sections - 1 - sec
    prev = jnp.maximum(sec - 1, 0)
    nxt = jnp.minimum(sec + 1, sections - 1)
    peers = [flipped(me, k) for k in range(ways)]
    rows_of = [pl.ds(pl.multiple_of(p * width, width), width) for p in peers]
    relay = ways == 4
    per_group = ways // KVH
    groups = [lax.div(p, per_group) for p in peers]
    pieces = PIECES if width % (PIECES * TILE) == 0 else 1
    piece_width = width // pieces
    piece_cols = [pl.ds(p * piece_width, piece_width) for p in range(pieces)]

    load_ow, load_kvw, load_qw = [
        pltpu.make_async_copy(a, b, wsem.at[i])
        for i, (a, b) in enumerate(((ow_hbm, ow), (kvw_hbm, kvw), (qw_hbm, qw)))
    ]
    for load in (load_ow, load_kvw, load_qw):
        load.start()

    used = []
    pending = []

    def send(src, dst, axis, peer, start=True):
        i = len(used)
        used.append(i)
        copy = pltpu.make_async_remote_copy(
            src_ref=src,
            dst_ref=dst,
            send_sem=ssem.at[i],
            recv_sem=rsem.at[i],
            device_id={axis: peer},
            device_id_type=pl.DeviceIdType.MESH,
        )
        if start:
            copy.start()
            pending.append(copy)
        return copy

    def to_peer(k, src, dst):
        return send(src, dst, "tensor", peers[k])

    barrier = pltpu.get_barrier_semaphore()

    def greet(axis, peer):
        pl.semaphore_signal(
            barrier, inc=1, device_id={axis: peer}, device_id_type=pl.DeviceIdType.MESH
        )

    for k in range(1, ways):
        greet("tensor", peers[k])
    greet("section", mirror)

    @pl.when(has_prev)
    def _():
        greet("section", prev)

    @pl.when(has_next)
    def _():
        greet("section", nxt)

    @pl.when(early)
    def _():
        trav[...] = x_ref[...]

    @pl.when(jnp.logical_not(early))
    def _():
        trav[...] = stash_ref[slot_ref[0]]

    cg[0] = cot_ref[...]

    eye = lax.broadcasted_iota(jnp.int32, (tokens, tokens), 0) == lax.broadcasted_iota(
        jnp.int32, (tokens, tokens), 1
    )
    step = 32

    def squares(rows_ref):
        sums = []
        for r in range(0, tokens, step):
            v = rows_ref[r : r + step, :].astype(f32)
            sums.append(jnp.sum(v * v, axis=-1, keepdims=True))
        return jnp.concatenate(sums, axis=0)

    def sum_put(column, buf):
        as_row = jnp.sum(jnp.where(eye, column, 0.0), axis=0, keepdims=True)
        buf[0] = jnp.broadcast_to(as_row, (SUMROWS, tokens))

    def sum_send(buf):
        return [to_peer(k, buf.at[0], buf.at[k]) for k in range(1, ways)]

    def sum_total(copies, buf):
        finish(copies)
        total = buf[0, 0:1, :]
        for k in range(1, ways):
            total = total + buf[k, 0:1, :]
        return jnp.sum(jnp.where(eye, total, 0.0), axis=1, keepdims=True)

    def normalize(rows_ref, out, total):
        factor = lax.rsqrt(total / model + norm_eps)
        for r in range(0, tokens, step):
            v = rows_ref[r : r + step, :].astype(f32)
            out[0, r : r + step, :] = (v * factor[r : r + step] * gain_ref[...]).astype(bf16)
        return factor

    sum_put(squares(x_ref), f_sum)
    pl.semaphore_wait(barrier, ways + jnp.minimum(sec, 1) + jnp.minimum(sections - 1 - sec, 1))

    def gather_start(buf):
        if relay:
            return [to_peer(k, buf.at[0], buf.at[k]) for k in (1, 2)]
        return [to_peer(k, buf.at[0], buf.at[k]) for k in range(1, ways)]

    def gather_pass_on(buf, copies):
        if not relay:
            finish(copies)
            return []
        copies[0].wait_recv()
        first = to_peer(2, buf.at[1, upper], buf.at[3, upper])
        copies[1].wait_recv()
        second = to_peer(1, buf.at[2, lower], buf.at[3, lower])
        return [first, second]

    def finish(copies):
        for copy in copies:
            copy.wait_recv()

    order = (3, 1, 2, 0) if relay else tuple(range(1, ways)) + (0,)

    def reduce_send(k, stage, land, cols):
        if k == 0:
            return []
        if not relay:
            return [to_peer(k, stage.at[k, :, cols], land.at[k, :, cols])]
        if k == 3:
            return [
                to_peer(1, stage.at[3, upper, cols], land.at[2, upper, cols]),
                to_peer(2, stage.at[3, lower, cols], land.at[1, lower, cols]),
            ]
        if k == 1:
            return [to_peer(1, stage.at[1, upper, cols], land.at[0, upper, cols])]
        return [to_peer(2, stage.at[2, lower, cols], land.at[0, lower, cols])]

    def reduce_pass_on(copies, part, stage, land, cols):
        if not relay:
            return copies
        copies[0].wait_recv()
        summed = part[2, upper, cols] + land[2, upper, cols].astype(f32)
        stage[2, upper, cols] = summed.astype(stage.dtype)
        first = to_peer(2, stage.at[2, upper, cols], land.at[3, upper, cols])
        copies[1].wait_recv()
        summed = part[1, lower, cols] + land[1, lower, cols].astype(f32)
        stage[1, lower, cols] = summed.astype(stage.dtype)
        second = to_peer(1, stage.at[1, lower, cols], land.at[3, lower, cols])
        return copies[2:] + [first, second]

    def reduced(part, land, rows, cols):
        total = part[0, rows, cols]
        for k in (0, 3) if relay else range(1, ways):
            total = total + land[k, rows, cols].astype(f32)
        return total

    kv_cols = pl.ds(0, 2 * HD)
    everything = pl.ds(0, tokens)

    def kv_terms(normed, part, land):
        copies = []
        for k in order:
            key_cols = pl.ds(pl.multiple_of(groups[k] * HD, HD), HD)
            value_cols = pl.ds(pl.multiple_of((KVH + groups[k]) * HD, HD), HD)
            part[k, :, 0:HD] = dot_nn(normed[0], kvw[:, key_cols])
            part[k, :, HD : 2 * HD] = dot_nn(normed[0], kvw[:, value_cols])
            copies += reduce_send(k, part, land, kv_cols)
        return copies

    def rotate(u):
        return u * cos_ref[...] + pltpu.roll(u, HD // 2, 1) * sin_ref[...]

    def unrotate(u):
        return u * cos_ref[...] - pltpu.roll(u, HD // 2, 1) * sin_ref[...]

    per_tile = TILE // HD
    scale = HD ** (-0.5)

    def accumulate(ks, buf, weight_tile, acc, out=None, finished=None):
        def body(n, carry):
            cols = pl.ds(pl.multiple_of(n * TILE, TILE), TILE)
            total = weight_tile(buf, ks[0], cols)
            for k in ks[1:]:
                total = total + weight_tile(buf, k, cols)
            if ks[0] != 0:
                total = total + acc[:, cols]
            acc[:, cols] = total
            if out is not None:
                for j in range(per_tile):
                    head = total[:, j * HD : (j + 1) * HD]
                    out[n * per_tile + j] = finished(head).astype(bf16)
            return carry

        lax.fori_loop(0, heads_here // per_tile, body, 0)

    def query_block(buf, k, cols):
        return dot_nn(buf[k], qw[rows_of[k], cols])

    def cot_block(buf, k, rows):
        return dot_nt(buf[k], ow[rows, rows_of[k]])

    def turned_query(head):
        return rotate(head) * scale

    def plain(head):
        return head

    near = [1, 2] if relay else list(range(1, ways // 2))
    far = [3] if relay else list(range(ways // 2, ways))

    def key_value(part, land):
        key_wide = reduced(part, land, everything, pl.ds(0, HD))
        value_wide = reduced(part, land, everything, pl.ds(HD, HD))
        return rotate(key_wide).astype(bf16), value_wide.astype(bf16), key_wide, value_wide

    span = PAIR * tokens
    position = lax.rem(lax.broadcasted_iota(jnp.int32, (span, tokens), 0), tokens)
    seen = position >= lax.broadcasted_iota(jnp.int32, (span, tokens), 1)

    def probabilities(q, key):
        scores = jnp.where(seen, dot_nt(q, key), -1e30)
        shifted = jnp.exp(scores - jnp.max(scores, axis=-1, keepdims=True))
        return shifted * (1.0 / jnp.sum(shifted, axis=-1, keepdims=True))

    def project(source, weight_tile, part, stage, land):
        copies = []
        tiles = piece_width // TILE
        for p in range(pieces):
            copies.append([])
            for k in order:

                def body(n, carry, k=k, p=p):
                    n = p * tiles + n
                    cols = pl.ds(pl.multiple_of(n * TILE, TILE), TILE)
                    value = weight_tile(source, k, n)
                    if not (relay and k == 3):
                        part[k, :, cols] = value
                    if k:
                        stage[k, :, cols] = value.astype(bf16)
                    return carry

                lax.fori_loop(0, tiles, body, 0)
                copies[p] += reduce_send(k, stage, land, piece_cols[p])
        return copies

    def out_tile(source, k, n):
        cols = pl.ds(pl.multiple_of(peers[k] * width + n * TILE, TILE), TILE)
        return dot_nn(source[...], ow[:, cols])

    def query_tile(source, k, n):
        rows = pl.ds(pl.multiple_of(peers[k] * width + n * TILE, TILE), TILE)
        return dot_nt(source[...], qw[rows, :])

    travel_copy = send(trav, travel_ref, "section", mirror)
    f_sums = sum_send(f_sum)
    c_copies = gather_start(cg)

    load_ow.wait()
    accumulate([0], cg, cot_block, c_acc)
    normalize(x_ref, fn, sum_total(f_sums, f_sum))
    load_kvw.wait()
    kvf = kv_terms(fn, kvf_p, kvf_r)
    c_copies = gather_pass_on(cg, c_copies)
    x_copies = gather_start(fn)
    accumulate(near, cg, cot_block, c_acc)
    kvf = reduce_pass_on(kvf, kvf_p, kvf_p, kvf_r, kv_cols)
    load_qw.wait()
    accumulate([0], fn, query_block, f_acc)

    travel_copy.wait_recv()

    @pl.when(early)
    def _():
        back[...] = travel_ref[...]

    @pl.when(jnp.logical_not(early))
    def _():
        back[...] = x_ref[...]

    sum_put(squares(back), b_sum)
    b_sums = sum_send(b_sum)
    finish(c_copies)
    accumulate(far, cg, cot_block, c_acc, go, plain)
    factor = normalize(back, bn, sum_total(b_sums, b_sum))
    kvb = kv_terms(bn, kvb_p, kvb_r)
    x_copies = gather_pass_on(fn, x_copies)
    b_copies = gather_start(bn)
    accumulate(near, fn, query_block, f_acc)
    kvb = reduce_pass_on(kvb, kvb_p, kvb_p, kvb_r, kv_cols)
    accumulate([0], bn, query_block, b_acc)
    finish(kvf)
    key, value, _, _ = key_value(kvf_p, kvf_r)
    finish(x_copies)
    accumulate(far, fn, query_block, f_acc, qf, turned_query)
    for i in range(heads_here // PAIR):
        q = qf[PAIR * i : PAIR * (i + 1)].reshape(span, HD)
        weights = probabilities(q, key).astype(bf16)
        result = dot_nn(weights, value).astype(bf16)
        for j in range(PAIR):
            head = PAIR * i + j
            att[:, head * HD : (head + 1) * HD] = result[j * tokens : (j + 1) * tokens]

    b_copies = gather_pass_on(bn, b_copies)
    outs = project(att, out_tile, out_p, out_s, out_r)
    accumulate(near, bn, query_block, b_acc)
    for p in range(pieces):
        outs[p] = reduce_pass_on(outs[p], out_p, out_s, out_r, piece_cols[p])
    finish(b_copies)
    accumulate(far, bn, query_block, b_acc, qb, turned_query)

    finish(kvb)
    key, value, key_wide, value_wide = key_value(kvb_p, kvb_r)
    grad_key = jnp.zeros((tokens, HD), f32)
    grad_value = jnp.zeros((tokens, HD), f32)
    mixed = jnp.zeros((tokens, HD), f32)
    for i in range(heads_here // PAIR):
        q = qb[PAIR * i : PAIR * (i + 1)].reshape(span, HD)
        g = go[PAIR * i : PAIR * (i + 1)].reshape(span, HD)
        probs = probabilities(q, key)
        grad_probs = dot_nt(g, value)
        delta = jnp.sum(probs * grad_probs, axis=-1, keepdims=True)
        grad_scores = (probs * (grad_probs - delta)).astype(bf16)
        grad_q = dot_nn(grad_scores, key)
        for j in range(PAIR):
            head = PAIR * i + j
            turned = (unrotate(grad_q[j * tokens : (j + 1) * tokens]) * scale).astype(bf16)
            gqb[:, head * HD : (head + 1) * HD] = turned
            mixed = mixed + turned.astype(f32) * b_acc[:, head * HD : (head + 1) * HD]
        grad_key = grad_key + dot_tn(grad_scores, q)
        grad_value = grad_value + dot_tn(probs.astype(bf16), g)
    grad_key = unrotate(grad_key).astype(gk_r.dtype)
    grad_value = grad_value.astype(gk_r.dtype)
    gk_r[0, :, 0:HD] = grad_key
    gk_r[0, :, HD : 2 * HD] = grad_value
    gk_copies = [to_peer(k, gk_r.at[0], gk_r.at[k]) for k in range(1, ways)]
    mixed = mixed + grad_key.astype(f32) * key_wide + grad_value.astype(f32) * value_wide
    sum_put(jnp.sum(mixed, axis=-1, keepdims=True), m_sum)
    m_sums = sum_send(m_sum)
    grads = project(gqb, query_tile, gq_p, gq_s, gq_r)

    next_copies = []
    grad_copies = []
    row_chunks = (upper, lower)

    for p in range(pieces):
        finish(outs[p])
        for rows in row_chunks:
            cols = piece_cols[p]
            total = reduced(out_p, out_r, rows, cols)
            lo[rows, cols] = (x_ref[rows, cols].astype(f32) + total).astype(bf16)
            copy = send(lo.at[rows, cols], next_ref.at[rows, cols], "section", nxt, start=False)
            pl.when(has_next)(copy.start)
            next_copies.append(copy)
        grads[p] = reduce_pass_on(grads[p], gq_p, gq_s, gq_r, piece_cols[p])

    finish(gk_copies)
    if per_group == 1:
        for k in range(ways):
            key_cols = pl.ds(pl.multiple_of(groups[k] * HD, HD), HD)
            value_cols = pl.ds(pl.multiple_of((KVH + groups[k]) * HD, HD), HD)
            gk_full[:, key_cols] = gk_r[k, :, 0:HD]
            gk_full[:, value_cols] = gk_r[k, :, HD : 2 * HD]
    else:
        gk_acc[...] = jnp.zeros_like(gk_acc)
        for k in range(ways):
            key_cols = pl.ds(pl.multiple_of(groups[k] * HD, HD), HD)
            value_cols = pl.ds(pl.multiple_of((KVH + groups[k]) * HD, HD), HD)
            gk_acc[:, key_cols] += gk_r[k, :, 0:HD].astype(f32)
            gk_acc[:, value_cols] += gk_r[k, :, HD : 2 * HD].astype(f32)
        gk_full[...] = gk_acc[...].astype(bf16)
    for n in range(width // TILE):
        cols = pl.ds(n * TILE, TILE)
        gq_p[0, :, cols] += dot_nt(gk_full[...], kvw[cols, :])
    square_mean = factor * factor * (sum_total(m_sums, m_sum) / model)

    for p in range(pieces):
        finish(grads[p])
        cols = piece_cols[p]
        for c, rows in enumerate(row_chunks):
            here = slice(c * half, (c + 1) * half)
            g = reduced(gq_p, gq_r, rows, cols) * gain_ref[:, cols]
            b = back[rows, cols].astype(f32)
            grad_rows = factor[here] * g - b * square_mean[here]
            gl[rows, cols] = (cot_ref[rows, cols].astype(f32) + grad_rows).astype(bf16)
            copy = send(gl.at[rows, cols], igrad_ref.at[rows, cols], "section", prev, start=False)
            pl.when(has_prev)(copy.start)
            grad_copies.append(copy)

    @pl.when(jnp.logical_not(has_prev))
    def _():
        next_ref[...] = jnp.zeros_like(next_ref)

    @pl.when(jnp.logical_not(has_next))
    def _():
        igrad_ref[...] = jnp.zeros_like(igrad_ref)

    for copy in pending:
        copy.wait_send()

    @pl.when(has_next)
    def _():
        for copy in next_copies:
            copy.wait_send()
        for copy in grad_copies:
            copy.wait_recv()

    @pl.when(has_prev)
    def _():
        for copy in next_copies:
            copy.wait_recv()
        for copy in grad_copies:
            copy.wait_send()


def hand_on(a, b, c, a_out, b_out, c_out, sem):
    copies = [
        pltpu.make_async_copy(src, dst, sem.at[i])
        for i, (src, dst) in enumerate(((a, a_out), (b, b_out), (c, c_out)))
    ]
    for copy in copies:
        copy.start()
    for copy in copies:
        copy.wait()


def copies_needed(ways):
    if ways == 4:
        return 1 + 9 + 3 * 4 + 2 * 6 + 2 * PIECES * 6 + 3 + 4 * PIECES
    return 1 + (ways - 1) * (3 + 3 + 2 + 2 * PIECES + 1) + 4 * PIECES


def per_device(
    ways,
    sections,
    section_input,
    stash_pool,
    reload_slot,
    cotangent,
    norm_gain,
    query_weight,
    kv_weight,
    out_weight,
):
    _, tokens, width = section_input.shape
    model = width * ways
    local = query_weight.shape[2]
    heads_here = local // HD
    cos_table, sin_table = rope_constants(tokens)
    grad_kv_type = bf16 if ways == KVH else f32
    copies = copies_needed(ways)
    vmem = pl.BlockSpec(memory_space=pltpu.VMEM)
    block = jax.ShapeDtypeStruct((tokens, width), bf16)
    gathered = pltpu.VMEM((ways, tokens, width), bf16)
    wide = pltpu.VMEM((ways, tokens, width), f32)
    kv_block = pltpu.VMEM((ways, tokens, 2 * HD), f32)
    head_block = pltpu.VMEM((heads_here, tokens, HD), bf16)
    flat = pltpu.VMEM((tokens, local), bf16)
    sums = pltpu.VMEM((ways, SUMROWS, tokens), f32)
    local_wide = pltpu.VMEM((tokens, local), f32)
    flat_block = pltpu.VMEM((tokens, width), bf16)
    scratch = [
        pltpu.VMEM((model, local), bf16),
        pltpu.VMEM((width, 2 * KVH * HD), bf16),
        pltpu.VMEM((local, model), bf16),
        gathered,
        gathered,
        gathered,
        flat_block,
        local_wide,
        local_wide,
        local_wide,
        head_block,
        head_block,
        head_block,
        flat,
        flat,
        kv_block,
        kv_block,
        kv_block,
        kv_block,
        wide,
        gathered,
        gathered,
        wide,
        gathered,
        gathered,
        pltpu.VMEM((ways, tokens, 2 * HD), grad_kv_type),
        pltpu.VMEM((tokens, 2 * KVH * HD), f32),
        pltpu.VMEM((tokens, 2 * KVH * HD), bf16),
        flat_block,
        flat_block,
        flat_block,
        sums,
        sums,
        sums,
        pltpu.SemaphoreType.DMA((3,)),
        pltpu.SemaphoreType.DMA((copies,)),
        pltpu.SemaphoreType.DMA((copies,)),
    ]
    macs = 5 * tokens * model * local + 3 * tokens * width * 2 * KVH * HD
    next_input, received, input_grad = pl.pallas_call(
        functools.partial(layer_kernel, ways, sections),
        out_shape=(block, block, block),
        in_specs=[pl.BlockSpec(memory_space=pltpu.SMEM)]
        + [vmem] * 6
        + [pl.BlockSpec(memory_space=pl.ANY)] * 3,
        out_specs=(vmem, vmem, vmem),
        scratch_shapes=scratch,
        cost_estimate=pl.CostEstimate(
            flops=2 * macs,
            bytes_accessed=2 * (2 * model * local + width * 2 * KVH * HD + 8 * tokens * width),
            transcendentals=2 * heads_here * tokens * tokens,
        ),
        compiler_params=pltpu.CompilerParams(
            collective_id=0, has_side_effects=True, vmem_limit_bytes=56 * 1024 * 1024
        ),
        name="attention_layer",
    )(
        reload_slot,
        section_input[0],
        stash_pool[0],
        cotangent[0],
        norm_gain,
        jnp.asarray(cos_table),
        jnp.asarray(sin_table),
        query_weight[0],
        kv_weight[0],
        out_weight[0],
    )
    anywhere = pl.BlockSpec(memory_space=pl.ANY)
    next_input, received, input_grad = pl.pallas_call(
        hand_on,
        out_shape=(block, block, block),
        in_specs=[anywhere] * 3,
        out_specs=(anywhere,) * 3,
        scratch_shapes=[pltpu.SemaphoreType.DMA((3,))],
        name="results",
    )(next_input, received, input_grad)
    return (next_input[None], received[None], input_grad[None])


def solution(mesh):
    return jax.shard_map(
        functools.partial(per_device, mesh.shape["tensor"], mesh.shape["section"]),
        mesh=mesh,
        in_specs=(
            P("section", "dp", "tensor"),
            P("section", None, "dp", "tensor"),
            P("section"),
            P("section", "dp", "tensor"),
            P("section", "tensor"),
            P("section", None, "tensor"),
            P("section", "tensor", None),
            P("section", "tensor", None),
        ),
        out_specs=(
            P("section", "dp", "tensor"),
            P("section", "dp", "tensor"),
            P("section", "dp", "tensor"),
        ),
        check_vma=False,
    )
```

```python
import functools

import jax
import jax.numpy as jnp
import numpy as np
from jax import lax
from jax.experimental import pallas as pl
from jax.experimental.pallas import tpu as pltpu
from jax.sharding import PartitionSpec as P

HEADS = 32
KVH = 4
HD = 128
PAIR = 2
TILE = 256
SUMROWS = 8
PIECES = 2

norm_eps = 1e-05
f32 = jnp.float32
bf16 = jnp.bfloat16


def rope_constants(tokens):
    half = HD // 2
    inverse = np.float32(10000.0) ** (
        np.float32(-2.0) * np.arange(half, dtype=np.float32) / np.float32(HD)
    )
    angles = np.arange(tokens, dtype=np.float32)[:, None] * inverse[None, :].astype(np.float32)
    cos, sin = np.cos(angles), np.sin(angles)
    return (
        np.concatenate([cos, cos], axis=1).astype(np.float32),
        np.concatenate([-sin, sin], axis=1).astype(np.float32),
    )


def flipped(index, bits):
    place = 1
    while place <= bits:
        if bits & place:
            bit = lax.rem(lax.div(index, place), 2)
            index = index + place * (1 - 2 * bit)
        place *= 2
    return index


def dot_nn(a, b):
    return jnp.dot(a, b, preferred_element_type=f32)


def dot_nt(a, b):
    return lax.dot_general(a, b, (((1,), (1,)), ((), ())), preferred_element_type=f32)


def dot_tn(a, b):
    return lax.dot_general(a, b, (((0,), (0,)), ((), ())), preferred_element_type=f32)


def layer_kernel(
    ways,
    sections,
    slot_ref,
    x_ref,
    stash_ref,
    cot_ref,
    gain_ref,
    cos_ref,
    sin_ref,
    qw_hbm,
    kvw_hbm,
    ow_hbm,
    next_ref,
    travel_ref,
    igrad_ref,
    qw,
    kvw,
    ow,
    cg,
    fn,
    bn,
    back,
    c_acc,
    f_acc,
    b_acc,
    qf,
    qb,
    go,
    att,
    gqb,
    kvf_p,
    kvf_r,
    kvb_p,
    kvb_r,
    out_p,
    out_s,
    out_r,
    gq_p,
    gq_s,
    gq_r,
    gk_r,
    gk_acc,
    gk_full,
    trav,
    lo,
    gl,
    f_sum,
    b_sum,
    m_sum,
    wsem,
    ssem,
    rsem,
):
    tokens, width = x_ref.shape
    heads_here = qw.shape[1] // HD
    model = width * ways
    half = tokens // 2
    upper, lower = pl.ds(0, half), pl.ds(half, half)
    me = lax.axis_index("tensor")
    sec = lax.axis_index("section")
    early = sec < sections // 2
    has_prev = sec > 0
    has_next = sec < sections - 1
    mirror = sections - 1 - sec
    prev = jnp.maximum(sec - 1, 0)
    nxt = jnp.minimum(sec + 1, sections - 1)
    peers = [flipped(me, k) for k in range(ways)]
    rows_of = [pl.ds(pl.multiple_of(p * width, width), width) for p in peers]
    relay = ways == 4
    per_group = ways // KVH
    groups = [lax.div(p, per_group) for p in peers]
    pieces = PIECES if width % (PIECES * TILE) == 0 else 1
    piece_width = width // pieces
    piece_cols = [pl.ds(p * piece_width, piece_width) for p in range(pieces)]

    load_kvw, load_qw, load_ow = [
        pltpu.make_async_copy(a, b, wsem.at[i])
        for i, (a, b) in enumerate(((kvw_hbm, kvw), (qw_hbm, qw), (ow_hbm, ow)))
    ]
    for load in (load_kvw, load_qw, load_ow):
        load.start()

    used = []
    pending = []

    def send(src, dst, axis, peer, start=True):
        i = len(used)
        used.append(i)
        copy = pltpu.make_async_remote_copy(
            src_ref=src,
            dst_ref=dst,
            send_sem=ssem.at[i],
            recv_sem=rsem.at[i],
            device_id={axis: peer},
            device_id_type=pl.DeviceIdType.MESH,
        )
        if start:
            copy.start()
            pending.append(copy)
        return copy

    def to_peer(k, src, dst):
        return send(src, dst, "tensor", peers[k])

    barrier = pltpu.get_barrier_semaphore()

    def greet(axis, peer):
        pl.semaphore_signal(
            barrier, inc=1, device_id={axis: peer}, device_id_type=pl.DeviceIdType.MESH
        )

    for k in range(1, ways):
        greet("tensor", peers[k])
    greet("section", mirror)

    @pl.when(has_prev)
    def _():
        greet("section", prev)

    @pl.when(has_next)
    def _():
        greet("section", nxt)

    @pl.when(early)
    def _():
        trav[...] = x_ref[...]

    @pl.when(jnp.logical_not(early))
    def _():
        trav[...] = stash_ref[slot_ref[0]]

    cg[0] = cot_ref[...]

    eye = lax.broadcasted_iota(jnp.int32, (tokens, tokens), 0) == lax.broadcasted_iota(
        jnp.int32, (tokens, tokens), 1
    )
    step = 32

    def squares(rows_ref):
        sums = []
        for r in range(0, tokens, step):
            v = rows_ref[r : r + step, :].astype(f32)
            sums.append(jnp.sum(v * v, axis=-1, keepdims=True))
        return jnp.concatenate(sums, axis=0)

    def sum_put(column, buf):
        as_row = jnp.sum(jnp.where(eye, column, 0.0), axis=0, keepdims=True)
        buf[0] = jnp.broadcast_to(as_row, (SUMROWS, tokens))

    def sum_send(buf):
        return [to_peer(k, buf.at[0], buf.at[k]) for k in range(1, ways)]

    def sum_total(copies, buf):
        finish(copies)
        total = buf[0, 0:1, :]
        for k in range(1, ways):
            total = total + buf[k, 0:1, :]
        return jnp.sum(jnp.where(eye, total, 0.0), axis=1, keepdims=True)

    def normalize(rows_ref, out, total):
        factor = lax.rsqrt(total / model + norm_eps)
        for r in range(0, tokens, step):
            v = rows_ref[r : r + step, :].astype(f32)
            out[0, r : r + step, :] = (v * factor[r : r + step] * gain_ref[...]).astype(bf16)
        return factor

    sum_put(squares(x_ref), f_sum)
    pl.semaphore_wait(barrier, ways + jnp.minimum(sec, 1) + jnp.minimum(sections - 1 - sec, 1))

    def gather_first(buf):
        if relay:
            return [
                to_peer(1, buf.at[0, upper], buf.at[1, upper]),
                to_peer(2, buf.at[0, lower], buf.at[2, lower]),
            ]
        return [to_peer(k, buf.at[0], buf.at[k]) for k in range(1, ways)]

    def gather_second(buf):
        if relay:
            return [
                to_peer(1, buf.at[0, lower], buf.at[1, lower]),
                to_peer(2, buf.at[0, upper], buf.at[2, upper]),
            ]
        return []

    def gather_pass_on(buf, copies):
        if not relay:
            finish(copies)
            return []
        copies[0].wait_recv()
        first = to_peer(2, buf.at[1, upper], buf.at[3, upper])
        copies[1].wait_recv()
        second = to_peer(1, buf.at[2, lower], buf.at[3, lower])
        return [first, second]

    def finish(copies):
        for copy in copies:
            copy.wait_recv()

    order = (3, 1, 2, 0) if relay else tuple(range(1, ways)) + (0,)

    def reduce_send(k, stage, land, cols):
        if k == 0:
            return []
        if not relay:
            return [to_peer(k, stage.at[k, :, cols], land.at[k, :, cols])]
        if k == 3:
            return [
                to_peer(1, stage.at[3, upper, cols], land.at[2, upper, cols]),
                to_peer(2, stage.at[3, lower, cols], land.at[1, lower, cols]),
            ]
        if k == 1:
            return [to_peer(1, stage.at[1, upper, cols], land.at[0, upper, cols])]
        return [to_peer(2, stage.at[2, lower, cols], land.at[0, lower, cols])]

    def reduce_pass_on(copies, part, stage, land, cols):
        if not relay:
            return copies
        copies[0].wait_recv()
        summed = part[2, upper, cols] + land[2, upper, cols].astype(f32)
        stage[2, upper, cols] = summed.astype(stage.dtype)
        first = to_peer(2, stage.at[2, upper, cols], land.at[3, upper, cols])
        copies[1].wait_recv()
        summed = part[1, lower, cols] + land[1, lower, cols].astype(f32)
        stage[1, lower, cols] = summed.astype(stage.dtype)
        second = to_peer(1, stage.at[1, lower, cols], land.at[3, lower, cols])
        return copies[2:] + [first, second]

    def reduced(part, land, rows, cols):
        total = part[0, rows, cols]
        for k in (0, 3) if relay else range(1, ways):
            total = total + land[k, rows, cols].astype(f32)
        return total

    def tile_loop(count, body):
        lax.fori_loop(0, count, body, 0, unroll=2 if count % 2 == 0 else 1)

    kv_cols = pl.ds(0, 2 * HD)
    all_cols = pl.ds(0, width)
    everything = pl.ds(0, tokens)

    def kv_terms(normed, part, land):
        copies = []
        for k in order:
            key_cols = pl.ds(pl.multiple_of(groups[k] * HD, HD), HD)
            value_cols = pl.ds(pl.multiple_of((KVH + groups[k]) * HD, HD), HD)
            part[k, :, 0:HD] = dot_nn(normed[0], kvw[:, key_cols])
            part[k, :, HD : 2 * HD] = dot_nn(normed[0], kvw[:, value_cols])
            copies += reduce_send(k, part, land, kv_cols)
        return copies

    def rotate(u):
        return u * cos_ref[...] + pltpu.roll(u, HD // 2, 1) * sin_ref[...]

    def unrotate(u):
        return u * cos_ref[...] - pltpu.roll(u, HD // 2, 1) * sin_ref[...]

    per_tile = TILE // HD
    scale = HD ** (-0.5)

    def accumulate(ks, buf, weight_tile, acc, out=None, finished=None):
        def body(n, carry):
            cols = pl.ds(pl.multiple_of(n * TILE, TILE), TILE)
            total = weight_tile(buf, ks[0], cols)
            for k in ks[1:]:
                total = total + weight_tile(buf, k, cols)
            if ks[0] != 0:
                total = total + acc[:, cols]
            acc[:, cols] = total
            if out is not None:
                for j in range(per_tile):
                    head = total[:, j * HD : (j + 1) * HD]
                    out[n * per_tile + j] = finished(head).astype(bf16)
            return carry

        tile_loop(heads_here // per_tile, body)

    def query_block(buf, k, cols):
        return dot_nn(buf[k], qw[rows_of[k], cols])

    def cot_block(buf, k, rows):
        return dot_nt(buf[k], ow[rows, rows_of[k]])

    def turned_query(head):
        return rotate(head) * scale

    def plain(head):
        return head

    near = [1, 2] if relay else list(range(1, ways // 2))
    far = [3] if relay else list(range(ways // 2, ways))

    def key_value(part, land):
        key_wide = reduced(part, land, everything, pl.ds(0, HD))
        value_wide = reduced(part, land, everything, pl.ds(HD, HD))
        return rotate(key_wide).astype(bf16), value_wide.astype(bf16), key_wide, value_wide

    span = PAIR * tokens
    position = lax.rem(lax.broadcasted_iota(jnp.int32, (span, tokens), 0), tokens)
    seen = position >= lax.broadcasted_iota(jnp.int32, (span, tokens), 1)

    def probabilities(q, key):
        scores = jnp.where(seen, dot_nt(q, key), -1e30)
        shifted = jnp.exp(scores - jnp.max(scores, axis=-1, keepdims=True))
        return shifted * (1.0 / jnp.sum(shifted, axis=-1, keepdims=True))

    def project(source, weight_tile, part, stage, k, first, count):
        def body(n, carry):
            n = first + n
            cols = pl.ds(pl.multiple_of(n * TILE, TILE), TILE)
            value = weight_tile(source, k, n)
            if not (relay and k == 3):
                part[k, :, cols] = value
            if k:
                stage[k, :, cols] = value.astype(bf16)
            return carry

        tile_loop(count, body)

    def out_tile(source, k, n):
        cols = pl.ds(pl.multiple_of(peers[k] * width + n * TILE, TILE), TILE)
        return dot_nn(source[...], ow[:, cols])

    def query_tile(source, k, n):
        rows = pl.ds(pl.multiple_of(peers[k] * width + n * TILE, TILE), TILE)
        return dot_nt(source[...], qw[rows, :])

    travel_copy = send(trav, travel_ref, "section", mirror)
    f_sums = sum_send(f_sum)
    c_first = gather_first(cg)
    normalize(x_ref, fn, sum_total(f_sums, f_sum))
    x_first = gather_first(fn)
    x_second = gather_second(fn)
    load_kvw.wait()
    kvf = kv_terms(fn, kvf_p, kvf_r)
    load_qw.wait()
    accumulate([0], fn, query_block, f_acc)
    x_far = gather_pass_on(fn, x_first)
    c_far = gather_pass_on(cg, c_first)
    c_second = gather_second(cg)
    kvf = reduce_pass_on(kvf, kvf_p, kvf_p, kvf_r, kv_cols)
    finish(x_second)
    accumulate(near, fn, query_block, f_acc)

    travel_copy.wait_recv()

    @pl.when(early)
    def _():
        back[...] = travel_ref[...]

    @pl.when(jnp.logical_not(early))
    def _():
        back[...] = x_ref[...]

    sum_put(squares(back), b_sum)
    b_sums = sum_send(b_sum)
    finish(x_far)
    accumulate(far, fn, query_block, f_acc, qf, turned_query)
    factor = normalize(back, bn, sum_total(b_sums, b_sum))
    b_first = gather_first(bn)
    b_second = gather_second(bn)
    kvb = kv_terms(bn, kvb_p, kvb_r)
    finish(kvf)
    key, value, _, _ = key_value(kvf_p, kvf_r)
    for i in range(heads_here // PAIR):
        q = qf[PAIR * i : PAIR * (i + 1)].reshape(span, HD)
        weights = probabilities(q, key).astype(bf16)
        result = dot_nn(weights, value).astype(bf16)
        for j in range(PAIR):
            head = PAIR * i + j
            att[:, head * HD : (head + 1) * HD] = result[j * tokens : (j + 1) * tokens]

    b_far = gather_pass_on(bn, b_first)
    load_ow.wait()
    outs = []
    for k in order:
        project(att, out_tile, out_p, out_s, k, 0, width // TILE)
        if k == order[0]:
            kvb = reduce_pass_on(kvb, kvb_p, kvb_p, kvb_r, kv_cols)
        outs += reduce_send(k, out_s, out_r, all_cols)
    finish(c_second)
    finish(c_far)
    accumulate(list(range(ways)), cg, cot_block, c_acc, go, plain)
    outs = reduce_pass_on(outs, out_p, out_s, out_r, all_cols)
    finish(b_second)
    finish(b_far)
    accumulate(list(range(ways)), bn, query_block, b_acc, qb, turned_query)

    finish(kvb)
    key, value, key_wide, value_wide = key_value(kvb_p, kvb_r)
    grad_key = jnp.zeros((tokens, HD), f32)
    grad_value = jnp.zeros((tokens, HD), f32)
    mixed = jnp.zeros((tokens, HD), f32)
    for i in range(heads_here // PAIR):
        q = qb[PAIR * i : PAIR * (i + 1)].reshape(span, HD)
        g = go[PAIR * i : PAIR * (i + 1)].reshape(span, HD)
        probs = probabilities(q, key)
        grad_probs = dot_nt(g, value)
        delta = jnp.sum(probs * grad_probs, axis=-1, keepdims=True)
        grad_scores = (probs * (grad_probs - delta)).astype(bf16)
        grad_q = dot_nn(grad_scores, key)
        for j in range(PAIR):
            head = PAIR * i + j
            turned = (unrotate(grad_q[j * tokens : (j + 1) * tokens]) * scale).astype(bf16)
            gqb[:, head * HD : (head + 1) * HD] = turned
            mixed = mixed + turned.astype(f32) * b_acc[:, head * HD : (head + 1) * HD]
        grad_key = grad_key + dot_tn(grad_scores, q)
        grad_value = grad_value + dot_tn(probs.astype(bf16), g)
    grad_key = unrotate(grad_key).astype(gk_r.dtype)
    grad_value = grad_value.astype(gk_r.dtype)
    gk_r[0, :, 0:HD] = grad_key
    gk_r[0, :, HD : 2 * HD] = grad_value
    gk_copies = [to_peer(k, gk_r.at[0], gk_r.at[k]) for k in range(1, ways)]
    mixed = mixed + grad_key.astype(f32) * key_wide + grad_value.astype(f32) * value_wide
    sum_put(jnp.sum(mixed, axis=-1, keepdims=True), m_sum)
    m_sums = sum_send(m_sum)
    grads = []
    piece_tiles = piece_width // TILE
    for p in range(pieces):
        grads.append([])
        for k in order:
            project(gqb, query_tile, gq_p, gq_s, k, p * piece_tiles, piece_tiles)
            grads[p] += reduce_send(k, gq_s, gq_r, piece_cols[p])

    next_copies = []
    grad_copies = []
    row_chunks = (upper, lower)

    finish(outs)
    for rows in row_chunks:
        total = reduced(out_p, out_r, rows, all_cols)
        lo[rows, :] = (x_ref[rows, :].astype(f32) + total).astype(bf16)
        copy = send(lo.at[rows], next_ref.at[rows], "section", nxt, start=False)
        pl.when(has_next)(copy.start)
        next_copies.append(copy)
    for p in range(pieces):
        grads[p] = reduce_pass_on(grads[p], gq_p, gq_s, gq_r, piece_cols[p])

    finish(gk_copies)
    if per_group == 1:
        for k in range(ways):
            key_cols = pl.ds(pl.multiple_of(groups[k] * HD, HD), HD)
            value_cols = pl.ds(pl.multiple_of((KVH + groups[k]) * HD, HD), HD)
            gk_full[:, key_cols] = gk_r[k, :, 0:HD]
            gk_full[:, value_cols] = gk_r[k, :, HD : 2 * HD]
    else:
        gk_acc[...] = jnp.zeros_like(gk_acc)
        for k in range(ways):
            key_cols = pl.ds(pl.multiple_of(groups[k] * HD, HD), HD)
            value_cols = pl.ds(pl.multiple_of((KVH + groups[k]) * HD, HD), HD)
            gk_acc[:, key_cols] += gk_r[k, :, 0:HD].astype(f32)
            gk_acc[:, value_cols] += gk_r[k, :, HD : 2 * HD].astype(f32)
        gk_full[...] = gk_acc[...].astype(bf16)
    for n in range(width // TILE):
        cols = pl.ds(n * TILE, TILE)
        gq_p[0, :, cols] += dot_nt(gk_full[...], kvw[cols, :])
    square_mean = factor * factor * (sum_total(m_sums, m_sum) / model)

    for p in range(pieces):
        finish(grads[p])
        cols = piece_cols[p]
        for c, rows in enumerate(row_chunks):
            here = slice(c * half, (c + 1) * half)
            g = reduced(gq_p, gq_r, rows, cols) * gain_ref[:, cols]
            b = back[rows, cols].astype(f32)
            grad_rows = factor[here] * g - b * square_mean[here]
            gl[rows, cols] = (cot_ref[rows, cols].astype(f32) + grad_rows).astype(bf16)
            copy = send(gl.at[rows, cols], igrad_ref.at[rows, cols], "section", prev, start=False)
            pl.when(has_prev)(copy.start)
            grad_copies.append(copy)

    @pl.when(jnp.logical_not(has_prev))
    def _():
        next_ref[...] = jnp.zeros_like(next_ref)

    @pl.when(jnp.logical_not(has_next))
    def _():
        igrad_ref[...] = jnp.zeros_like(igrad_ref)

    for copy in pending:
        copy.wait_send()

    @pl.when(has_next)
    def _():
        for copy in next_copies:
            copy.wait_send()
        for copy in grad_copies:
            copy.wait_recv()

    @pl.when(has_prev)
    def _():
        for copy in next_copies:
            copy.wait_recv()
        for copy in grad_copies:
            copy.wait_send()


def hand_on(a, b, c, a_out, b_out, c_out):
    a_out[...] = a[...]
    b_out[...] = b[...]
    c_out[...] = c[...]


def copies_needed(ways):
    if ways == 4:
        return 1 + 9 + 3 * 6 + 2 * 6 + 6 + PIECES * 6 + 3 + 2 + 2 * PIECES
    return 1 + (ways - 1) * (3 + 3 + 2 + 2 * PIECES + 1) + 4 * PIECES


def per_device(
    ways,
    sections,
    section_input,
    stash_pool,
    reload_slot,
    cotangent,
    norm_gain,
    query_weight,
    kv_weight,
    out_weight,
):
    _, tokens, width = section_input.shape
    model = width * ways
    local = query_weight.shape[2]
    heads_here = local // HD
    cos_table, sin_table = rope_constants(tokens)
    grad_kv_type = bf16 if ways == KVH else f32
    copies = copies_needed(ways)
    vmem = pl.BlockSpec(memory_space=pltpu.VMEM)
    block = jax.ShapeDtypeStruct((tokens, width), bf16)
    gathered = pltpu.VMEM((ways, tokens, width), bf16)
    wide = pltpu.VMEM((ways, tokens, width), f32)
    kv_block = pltpu.VMEM((ways, tokens, 2 * HD), f32)
    head_block = pltpu.VMEM((heads_here, tokens, HD), bf16)
    flat = pltpu.VMEM((tokens, local), bf16)
    sums = pltpu.VMEM((ways, SUMROWS, tokens), f32)
    local_wide = pltpu.VMEM((tokens, local), f32)
    flat_block = pltpu.VMEM((tokens, width), bf16)
    scratch = [
        pltpu.VMEM((model, local), bf16),
        pltpu.VMEM((width, 2 * KVH * HD), bf16),
        pltpu.VMEM((local, model), bf16),
        gathered,
        gathered,
        gathered,
        flat_block,
        local_wide,
        local_wide,
        local_wide,
        head_block,
        head_block,
        head_block,
        flat,
        flat,
        kv_block,
        kv_block,
        kv_block,
        kv_block,
        wide,
        gathered,
        gathered,
        wide,
        gathered,
        gathered,
        pltpu.VMEM((ways, tokens, 2 * HD), grad_kv_type),
        pltpu.VMEM((tokens, 2 * KVH * HD), f32),
        pltpu.VMEM((tokens, 2 * KVH * HD), bf16),
        flat_block,
        flat_block,
        flat_block,
        sums,
        sums,
        sums,
        pltpu.SemaphoreType.DMA((3,)),
        pltpu.SemaphoreType.DMA((copies,)),
        pltpu.SemaphoreType.DMA((copies,)),
    ]
    macs = 5 * tokens * model * local + 3 * tokens * width * 2 * KVH * HD
    next_input, received, input_grad = pl.pallas_call(
        functools.partial(layer_kernel, ways, sections),
        out_shape=(block, block, block),
        in_specs=[pl.BlockSpec(memory_space=pltpu.SMEM)]
        + [vmem] * 6
        + [pl.BlockSpec(memory_space=pl.ANY)] * 3,
        out_specs=(vmem, vmem, vmem),
        scratch_shapes=scratch,
        cost_estimate=pl.CostEstimate(
            flops=2 * macs,
            bytes_accessed=2 * (2 * model * local + width * 2 * KVH * HD + 8 * tokens * width),
            transcendentals=2 * heads_here * tokens * tokens,
        ),
        compiler_params=pltpu.CompilerParams(
            collective_id=0, has_side_effects=True, vmem_limit_bytes=56 * 1024 * 1024
        ),
        name="attention_layer",
    )(
        reload_slot,
        section_input[0],
        stash_pool[0],
        cotangent[0],
        norm_gain,
        jnp.asarray(cos_table),
        jnp.asarray(sin_table),
        query_weight[0],
        kv_weight[0],
        out_weight[0],
    )
    next_input, received, input_grad = pl.pallas_call(
        hand_on,
        out_shape=(block, block, block),
        in_specs=[vmem] * 3,
        out_specs=(vmem,) * 3,
        name="results",
    )(next_input, received, input_grad)
    return (next_input[None], received[None], input_grad[None])


def solution(mesh):
    return jax.shard_map(
        functools.partial(per_device, mesh.shape["tensor"], mesh.shape["section"]),
        mesh=mesh,
        in_specs=(
            P("section", "dp", "tensor"),
            P("section", None, "dp", "tensor"),
            P("section"),
            P("section", "dp", "tensor"),
            P("section", "tensor"),
            P("section", None, "tensor"),
            P("section", "tensor", None),
            P("section", "tensor", None),
        ),
        out_specs=(
            P("section", "dp", "tensor"),
            P("section", "dp", "tensor"),
            P("section", "dp", "tensor"),
        ),
        check_vma=False,
    )
```

```python
import functools

import jax
import jax.numpy as jnp
import numpy as np
from jax import lax
from jax.experimental import pallas as pl
from jax.experimental.pallas import tpu as pltpu
from jax.sharding import PartitionSpec as P

HEADS = 32
KVH = 4
HD = 128
PAIR = 2
TILE = 256
SUMROWS = 8
PIECES = 2

norm_eps = 1e-05
f32 = jnp.float32
bf16 = jnp.bfloat16


def rope_constants(tokens):
    half = HD // 2
    inverse = np.float32(10000.0) ** (
        np.float32(-2.0) * np.arange(half, dtype=np.float32) / np.float32(HD)
    )
    angles = np.arange(tokens, dtype=np.float32)[:, None] * inverse[None, :].astype(np.float32)
    cos, sin = np.cos(angles), np.sin(angles)
    return (
        np.concatenate([cos, cos], axis=1).astype(np.float32),
        np.concatenate([-sin, sin], axis=1).astype(np.float32),
    )


def flipped(index, bits):
    place = 1
    while place <= bits:
        if bits & place:
            bit = lax.rem(lax.div(index, place), 2)
            index = index + place * (1 - 2 * bit)
        place *= 2
    return index


def dot_nn(a, b):
    return jnp.dot(a, b, preferred_element_type=f32)


def dot_nt(a, b):
    return lax.dot_general(a, b, (((1,), (1,)), ((), ())), preferred_element_type=f32)


def dot_tn(a, b):
    return lax.dot_general(a, b, (((0,), (0,)), ((), ())), preferred_element_type=f32)


def layer_kernel(
    ways,
    sections,
    slot_ref,
    x_ref,
    stash_ref,
    cot_ref,
    gain_ref,
    cos_ref,
    sin_ref,
    qw_hbm,
    kvw_hbm,
    ow_hbm,
    next_ref,
    travel_ref,
    igrad_ref,
    qw,
    kvw,
    ow,
    cg,
    fn,
    bn,
    back,
    c_acc,
    f_acc,
    b_acc,
    qf,
    qb,
    go,
    att,
    gqb,
    kvf_p,
    kvf_r,
    kvb_p,
    kvb_r,
    out_p,
    out_s,
    out_r,
    gq_p,
    gq_s,
    gq_r,
    gk_r,
    gk_acc,
    gk_full,
    trav,
    lo,
    gl,
    f_sum,
    b_sum,
    m_sum,
    wsem,
    ssem,
    rsem,
):
    tokens, width = x_ref.shape
    heads_here = qw.shape[1] // HD
    model = width * ways
    half = tokens // 2
    upper, lower = pl.ds(0, half), pl.ds(half, half)
    me = lax.axis_index("tensor")
    sec = lax.axis_index("section")
    early = sec < sections // 2
    has_prev = sec > 0
    has_next = sec < sections - 1
    mirror = sections - 1 - sec
    prev = jnp.maximum(sec - 1, 0)
    nxt = jnp.minimum(sec + 1, sections - 1)
    peers = [flipped(me, k) for k in range(ways)]
    rows_of = [pl.ds(pl.multiple_of(p * width, width), width) for p in peers]
    relay = ways == 4
    per_group = ways // KVH
    groups = [lax.div(p, per_group) for p in peers]
    pieces = PIECES if width % (PIECES * TILE) == 0 else 1
    piece_width = width // pieces
    piece_cols = [pl.ds(p * piece_width, piece_width) for p in range(pieces)]

    load_kvw, load_qw, load_ow = [
        pltpu.make_async_copy(a, b, wsem.at[i])
        for i, (a, b) in enumerate(((kvw_hbm, kvw), (qw_hbm, qw), (ow_hbm, ow)))
    ]
    for load in (load_kvw, load_qw, load_ow):
        load.start()

    used = []
    pending = []

    def send(src, dst, axis, peer, start=True):
        i = len(used)
        used.append(i)
        copy = pltpu.make_async_remote_copy(
            src_ref=src,
            dst_ref=dst,
            send_sem=ssem.at[i],
            recv_sem=rsem.at[i],
            device_id={axis: peer},
            device_id_type=pl.DeviceIdType.MESH,
        )
        if start:
            copy.start()
            pending.append(copy)
        return copy

    def to_peer(k, src, dst):
        return send(src, dst, "tensor", peers[k])

    barrier = pltpu.get_barrier_semaphore()

    def greet(axis, peer):
        pl.semaphore_signal(
            barrier, inc=1, device_id={axis: peer}, device_id_type=pl.DeviceIdType.MESH
        )

    for k in range(1, ways):
        greet("tensor", peers[k])
    greet("section", mirror)

    @pl.when(has_prev)
    def _():
        greet("section", prev)

    @pl.when(has_next)
    def _():
        greet("section", nxt)

    @pl.when(early)
    def _():
        trav[...] = x_ref[...]

    @pl.when(jnp.logical_not(early))
    def _():
        trav[...] = stash_ref[slot_ref[0]]

    cg[0] = cot_ref[...]

    eye = lax.broadcasted_iota(jnp.int32, (tokens, tokens), 0) == lax.broadcasted_iota(
        jnp.int32, (tokens, tokens), 1
    )
    step = 32

    def squares(rows_ref):
        sums = []
        for r in range(0, tokens, step):
            v = rows_ref[r : r + step, :].astype(f32)
            sums.append(jnp.sum(v * v, axis=-1, keepdims=True))
        return jnp.concatenate(sums, axis=0)

    def sum_put(column, buf):
        as_row = jnp.sum(jnp.where(eye, column, 0.0), axis=0, keepdims=True)
        buf[0] = jnp.broadcast_to(as_row, (SUMROWS, tokens))

    def sum_send(buf):
        return [to_peer(k, buf.at[0], buf.at[k]) for k in range(1, ways)]

    def sum_total(copies, buf):
        finish(copies)
        total = buf[0, 0:1, :]
        for k in range(1, ways):
            total = total + buf[k, 0:1, :]
        return jnp.sum(jnp.where(eye, total, 0.0), axis=1, keepdims=True)

    def normalize(rows_ref, out, total):
        factor = lax.rsqrt(total / model + norm_eps)
        for r in range(0, tokens, step):
            v = rows_ref[r : r + step, :].astype(f32)
            out[0, r : r + step, :] = (v * factor[r : r + step] * gain_ref[...]).astype(bf16)
        return factor

    sum_put(squares(x_ref), f_sum)
    pl.semaphore_wait(barrier, ways + jnp.minimum(sec, 1) + jnp.minimum(sections - 1 - sec, 1))

    def gather_first(buf):
        if relay:
            return [
                to_peer(1, buf.at[0, upper], buf.at[1, upper]),
                to_peer(2, buf.at[0, lower], buf.at[2, lower]),
            ]
        return [to_peer(k, buf.at[0], buf.at[k]) for k in range(1, ways)]

    def gather_second(buf):
        if relay:
            return [
                to_peer(1, buf.at[0, lower], buf.at[1, lower]),
                to_peer(2, buf.at[0, upper], buf.at[2, upper]),
            ]
        return []

    def gather_pass_on(buf, copies):
        if not relay:
            finish(copies)
            return []
        copies[0].wait_recv()
        first = to_peer(2, buf.at[1, upper], buf.at[3, upper])
        copies[1].wait_recv()
        second = to_peer(1, buf.at[2, lower], buf.at[3, lower])
        return [first, second]

    def finish(copies):
        for copy in copies:
            copy.wait_recv()

    order = (3, 1, 2, 0) if relay else tuple(range(1, ways)) + (0,)

    def reduce_send(k, stage, land, cols):
        if k == 0:
            return []
        if not relay:
            return [to_peer(k, stage.at[k, :, cols], land.at[k, :, cols])]
        if k == 3:
            return [
                to_peer(1, stage.at[3, upper, cols], land.at[2, upper, cols]),
                to_peer(2, stage.at[3, lower, cols], land.at[1, lower, cols]),
            ]
        if k == 1:
            return [to_peer(1, stage.at[1, upper, cols], land.at[0, upper, cols])]
        return [to_peer(2, stage.at[2, lower, cols], land.at[0, lower, cols])]

    def reduce_pass_on(copies, part, stage, land, cols):
        if not relay:
            return copies
        copies[0].wait_recv()
        summed = part[2, upper, cols] + land[2, upper, cols].astype(f32)
        stage[2, upper, cols] = summed.astype(stage.dtype)
        first = to_peer(2, stage.at[2, upper, cols], land.at[3, upper, cols])
        copies[1].wait_recv()
        summed = part[1, lower, cols] + land[1, lower, cols].astype(f32)
        stage[1, lower, cols] = summed.astype(stage.dtype)
        second = to_peer(1, stage.at[1, lower, cols], land.at[3, lower, cols])
        return copies[2:] + [first, second]

    def reduced(part, land, rows, cols):
        total = part[0, rows, cols]
        for k in (0, 3) if relay else range(1, ways):
            total = total + land[k, rows, cols].astype(f32)
        return total

    def tile_loop(count, body):
        lax.fori_loop(0, count, body, 0, unroll=2 if count % 2 == 0 else 1)

    kv_cols = pl.ds(0, 2 * HD)
    all_cols = pl.ds(0, width)
    everything = pl.ds(0, tokens)

    def kv_terms(normed, part, land):
        copies = []
        for k in order:
            key_cols = pl.ds(pl.multiple_of(groups[k] * HD, HD), HD)
            value_cols = pl.ds(pl.multiple_of((KVH + groups[k]) * HD, HD), HD)
            part[k, :, 0:HD] = dot_nn(normed[0], kvw[:, key_cols])
            part[k, :, HD : 2 * HD] = dot_nn(normed[0], kvw[:, value_cols])
            copies += reduce_send(k, part, land, kv_cols)
        return copies

    def rotate(u):
        return u * cos_ref[...] + pltpu.roll(u, HD // 2, 1) * sin_ref[...]

    def unrotate(u):
        return u * cos_ref[...] - pltpu.roll(u, HD // 2, 1) * sin_ref[...]

    per_tile = TILE // HD
    scale = HD ** (-0.5)

    def accumulate(ks, buf, weight_tile, acc, out=None, finished=None):
        def body(n, carry):
            cols = pl.ds(pl.multiple_of(n * TILE, TILE), TILE)
            total = weight_tile(buf, ks[0], cols)
            for k in ks[1:]:
                total = total + weight_tile(buf, k, cols)
            if ks[0] != 0:
                total = total + acc[:, cols]
            acc[:, cols] = total
            if out is not None:
                for j in range(per_tile):
                    head = total[:, j * HD : (j + 1) * HD]
                    out[n * per_tile + j] = finished(head).astype(bf16)
            return carry

        tile_loop(heads_here // per_tile, body)

    def query_block(buf, k, cols):
        return dot_nn(buf[k], qw[rows_of[k], cols])

    def cot_block(buf, k, rows):
        return dot_nt(buf[k], ow[rows, rows_of[k]])

    def turned_query(head):
        return rotate(head) * scale

    def plain(head):
        return head

    near = [1, 2] if relay else list(range(1, ways // 2))
    far = [3] if relay else list(range(ways // 2, ways))

    def key_value(part, land):
        key_wide = reduced(part, land, everything, pl.ds(0, HD))
        value_wide = reduced(part, land, everything, pl.ds(HD, HD))
        return rotate(key_wide).astype(bf16), value_wide.astype(bf16), key_wide, value_wide

    span = PAIR * tokens
    position = lax.rem(lax.broadcasted_iota(jnp.int32, (span, tokens), 0), tokens)
    seen = position >= lax.broadcasted_iota(jnp.int32, (span, tokens), 1)

    def probabilities(q, key):
        scores = jnp.where(seen, dot_nt(q, key), -1e30)
        shifted = jnp.exp(scores - jnp.max(scores, axis=-1, keepdims=True))
        return shifted * (1.0 / jnp.sum(shifted, axis=-1, keepdims=True))

    def project(source, weight_tile, part, stage, k, first, count):
        def body(n, carry):
            n = first + n
            cols = pl.ds(pl.multiple_of(n * TILE, TILE), TILE)
            value = weight_tile(source, k, n)
            if not (relay and k == 3):
                part[k, :, cols] = value
            if k:
                stage[k, :, cols] = value.astype(bf16)
            return carry

        tile_loop(count, body)

    def out_tile(source, k, n):
        cols = pl.ds(pl.multiple_of(peers[k] * width + n * TILE, TILE), TILE)
        return dot_nn(source[...], ow[:, cols])

    def query_tile(source, k, n):
        rows = pl.ds(pl.multiple_of(peers[k] * width + n * TILE, TILE), TILE)
        return dot_nt(source[...], qw[rows, :])

    travel_copy = send(trav, travel_ref, "section", mirror)
    f_sums = sum_send(f_sum)
    c_first = gather_first(cg)
    normalize(x_ref, fn, sum_total(f_sums, f_sum))
    x_first = gather_first(fn)
    x_second = gather_second(fn)
    load_kvw.wait()
    kvf = kv_terms(fn, kvf_p, kvf_r)
    load_qw.wait()
    accumulate([0], fn, query_block, f_acc)
    x_far = gather_pass_on(fn, x_first)
    c_far = gather_pass_on(cg, c_first)
    c_second = gather_second(cg)
    kvf = reduce_pass_on(kvf, kvf_p, kvf_p, kvf_r, kv_cols)
    finish(x_second)
    accumulate(near, fn, query_block, f_acc)

    travel_copy.wait_recv()

    @pl.when(early)
    def _():
        back[...] = travel_ref[...]

    @pl.when(jnp.logical_not(early))
    def _():
        back[...] = x_ref[...]

    sum_put(squares(back), b_sum)
    b_sums = sum_send(b_sum)
    finish(x_far)
    accumulate(far, fn, query_block, f_acc, qf, turned_query)
    factor = normalize(back, bn, sum_total(b_sums, b_sum))
    b_first = gather_first(bn)
    b_second = gather_second(bn)
    kvb = kv_terms(bn, kvb_p, kvb_r)
    finish(kvf)
    key, value, _, _ = key_value(kvf_p, kvf_r)
    for i in range(heads_here // PAIR):
        q = qf[PAIR * i : PAIR * (i + 1)].reshape(span, HD)
        weights = probabilities(q, key).astype(bf16)
        result = dot_nn(weights, value).astype(bf16)
        for j in range(PAIR):
            head = PAIR * i + j
            att[:, head * HD : (head + 1) * HD] = result[j * tokens : (j + 1) * tokens]

    b_far = gather_pass_on(bn, b_first)
    load_ow.wait()
    for k in order:
        project(att, out_tile, out_p, out_s, k, 0, width // TILE)
    kvb = reduce_pass_on(kvb, kvb_p, kvb_p, kvb_r, kv_cols)
    finish(c_second)
    finish(c_far)
    accumulate(list(range(ways)), cg, cot_block, c_acc, go, plain)
    finish(b_second)
    accumulate([0] + near, bn, query_block, b_acc)
    finish(b_far)
    outs = []
    for k in order:
        outs += reduce_send(k, out_s, out_r, all_cols)
    accumulate(far, bn, query_block, b_acc, qb, turned_query)

    finish(kvb)
    key, value, key_wide, value_wide = key_value(kvb_p, kvb_r)
    grad_key = jnp.zeros((tokens, HD), f32)
    grad_value = jnp.zeros((tokens, HD), f32)
    mixed = jnp.zeros((tokens, HD), f32)
    for i in range(heads_here // PAIR):
        if i == heads_here // PAIR // 2:
            outs = reduce_pass_on(outs, out_p, out_s, out_r, all_cols)
        q = qb[PAIR * i : PAIR * (i + 1)].reshape(span, HD)
        g = go[PAIR * i : PAIR * (i + 1)].reshape(span, HD)
        probs = probabilities(q, key)
        grad_probs = dot_nt(g, value)
        delta = jnp.sum(probs * grad_probs, axis=-1, keepdims=True)
        grad_scores = (probs * (grad_probs - delta)).astype(bf16)
        grad_q = dot_nn(grad_scores, key)
        for j in range(PAIR):
            head = PAIR * i + j
            turned = (unrotate(grad_q[j * tokens : (j + 1) * tokens]) * scale).astype(bf16)
            gqb[:, head * HD : (head + 1) * HD] = turned
            mixed = mixed + turned.astype(f32) * b_acc[:, head * HD : (head + 1) * HD]
        grad_key = grad_key + dot_tn(grad_scores, q)
        grad_value = grad_value + dot_tn(probs.astype(bf16), g)
    grad_key = unrotate(grad_key).astype(gk_r.dtype)
    grad_value = grad_value.astype(gk_r.dtype)
    gk_r[0, :, 0:HD] = grad_key
    gk_r[0, :, HD : 2 * HD] = grad_value
    gk_copies = [to_peer(k, gk_r.at[0], gk_r.at[k]) for k in range(1, ways)]
    mixed = mixed + grad_key.astype(f32) * key_wide + grad_value.astype(f32) * value_wide
    sum_put(jnp.sum(mixed, axis=-1, keepdims=True), m_sum)
    m_sums = sum_send(m_sum)
    grads = []
    piece_tiles = piece_width // TILE
    for p in range(pieces):
        grads.append([])
        for k in order:
            project(gqb, query_tile, gq_p, gq_s, k, p * piece_tiles, piece_tiles)
            grads[p] += reduce_send(k, gq_s, gq_r, piece_cols[p])

    next_copies = []
    grad_copies = []
    row_chunks = (upper, lower)

    finish(outs)
    for rows in row_chunks:
        total = reduced(out_p, out_r, rows, all_cols)
        lo[rows, :] = (x_ref[rows, :].astype(f32) + total).astype(bf16)
        copy = send(lo.at[rows], next_ref.at[rows], "section", nxt, start=False)
        pl.when(has_next)(copy.start)
        next_copies.append(copy)
    for p in range(pieces):
        grads[p] = reduce_pass_on(grads[p], gq_p, gq_s, gq_r, piece_cols[p])

    finish(gk_copies)
    if per_group == 1:
        for k in range(ways):
            key_cols = pl.ds(pl.multiple_of(groups[k] * HD, HD), HD)
            value_cols = pl.ds(pl.multiple_of((KVH + groups[k]) * HD, HD), HD)
            gk_full[:, key_cols] = gk_r[k, :, 0:HD]
            gk_full[:, value_cols] = gk_r[k, :, HD : 2 * HD]
    else:
        gk_acc[...] = jnp.zeros_like(gk_acc)
        for k in range(ways):
            key_cols = pl.ds(pl.multiple_of(groups[k] * HD, HD), HD)
            value_cols = pl.ds(pl.multiple_of((KVH + groups[k]) * HD, HD), HD)
            gk_acc[:, key_cols] += gk_r[k, :, 0:HD].astype(f32)
            gk_acc[:, value_cols] += gk_r[k, :, HD : 2 * HD].astype(f32)
        gk_full[...] = gk_acc[...].astype(bf16)
    for n in range(width // TILE):
        cols = pl.ds(n * TILE, TILE)
        gq_p[0, :, cols] += dot_nt(gk_full[...], kvw[cols, :])
    square_mean = factor * factor * (sum_total(m_sums, m_sum) / model)

    for p in range(pieces):
        finish(grads[p])
        cols = piece_cols[p]
        for c, rows in enumerate(row_chunks):
            here = slice(c * half, (c + 1) * half)
            g = reduced(gq_p, gq_r, rows, cols) * gain_ref[:, cols]
            b = back[rows, cols].astype(f32)
            grad_rows = factor[here] * g - b * square_mean[here]
            gl[rows, cols] = (cot_ref[rows, cols].astype(f32) + grad_rows).astype(bf16)
            copy = send(gl.at[rows, cols], igrad_ref.at[rows, cols], "section", prev, start=False)
            pl.when(has_prev)(copy.start)
            grad_copies.append(copy)

    @pl.when(jnp.logical_not(has_prev))
    def _():
        next_ref[...] = jnp.zeros_like(next_ref)

    @pl.when(jnp.logical_not(has_next))
    def _():
        igrad_ref[...] = jnp.zeros_like(igrad_ref)

    for copy in pending:
        copy.wait_send()

    @pl.when(has_next)
    def _():
        for copy in next_copies:
            copy.wait_send()
        for copy in grad_copies:
            copy.wait_recv()

    @pl.when(has_prev)
    def _():
        for copy in next_copies:
            copy.wait_recv()
        for copy in grad_copies:
            copy.wait_send()


def hand_on(a, b, c, a_out, b_out, c_out):
    a_out[...] = a[...]
    b_out[...] = b[...]
    c_out[...] = c[...]


def copies_needed(ways):
    if ways == 4:
        return 1 + 9 + 3 * 6 + 2 * 6 + 6 + PIECES * 6 + 3 + 2 + 2 * PIECES
    return 1 + (ways - 1) * (3 + 3 + 2 + 2 * PIECES + 1) + 4 * PIECES


def per_device(
    ways,
    sections,
    section_input,
    stash_pool,
    reload_slot,
    cotangent,
    norm_gain,
    query_weight,
    kv_weight,
    out_weight,
):
    _, tokens, width = section_input.shape
    model = width * ways
    local = query_weight.shape[2]
    heads_here = local // HD
    cos_table, sin_table = rope_constants(tokens)
    grad_kv_type = bf16 if ways == KVH else f32
    copies = copies_needed(ways)
    vmem = pl.BlockSpec(memory_space=pltpu.VMEM)
    block = jax.ShapeDtypeStruct((tokens, width), bf16)
    gathered = pltpu.VMEM((ways, tokens, width), bf16)
    wide = pltpu.VMEM((ways, tokens, width), f32)
    kv_block = pltpu.VMEM((ways, tokens, 2 * HD), f32)
    head_block = pltpu.VMEM((heads_here, tokens, HD), bf16)
    flat = pltpu.VMEM((tokens, local), bf16)
    sums = pltpu.VMEM((ways, SUMROWS, tokens), f32)
    local_wide = pltpu.VMEM((tokens, local), f32)
    flat_block = pltpu.VMEM((tokens, width), bf16)
    scratch = [
        pltpu.VMEM((model, local), bf16),
        pltpu.VMEM((width, 2 * KVH * HD), bf16),
        pltpu.VMEM((local, model), bf16),
        gathered,
        gathered,
        gathered,
        flat_block,
        local_wide,
        local_wide,
        local_wide,
        head_block,
        head_block,
        head_block,
        flat,
        flat,
        kv_block,
        kv_block,
        kv_block,
        kv_block,
        wide,
        gathered,
        gathered,
        wide,
        gathered,
        gathered,
        pltpu.VMEM((ways, tokens, 2 * HD), grad_kv_type),
        pltpu.VMEM((tokens, 2 * KVH * HD), f32),
        pltpu.VMEM((tokens, 2 * KVH * HD), bf16),
        flat_block,
        flat_block,
        flat_block,
        sums,
        sums,
        sums,
        pltpu.SemaphoreType.DMA((3,)),
        pltpu.SemaphoreType.DMA((copies,)),
        pltpu.SemaphoreType.DMA((copies,)),
    ]
    macs = 5 * tokens * model * local + 3 * tokens * width * 2 * KVH * HD
    next_input, received, input_grad = pl.pallas_call(
        functools.partial(layer_kernel, ways, sections),
        out_shape=(block, block, block),
        in_specs=[pl.BlockSpec(memory_space=pltpu.SMEM)]
        + [vmem] * 6
        + [pl.BlockSpec(memory_space=pl.ANY)] * 3,
        out_specs=(vmem, vmem, vmem),
        scratch_shapes=scratch,
        cost_estimate=pl.CostEstimate(
            flops=2 * macs,
            bytes_accessed=2 * (2 * model * local + width * 2 * KVH * HD + 8 * tokens * width),
            transcendentals=2 * heads_here * tokens * tokens,
        ),
        compiler_params=pltpu.CompilerParams(
            collective_id=0, has_side_effects=True, vmem_limit_bytes=56 * 1024 * 1024
        ),
        name="attention_layer",
    )(
        reload_slot,
        section_input[0],
        stash_pool[0],
        cotangent[0],
        norm_gain,
        jnp.asarray(cos_table),
        jnp.asarray(sin_table),
        query_weight[0],
        kv_weight[0],
        out_weight[0],
    )
    next_input, received, input_grad = pl.pallas_call(
        hand_on,
        out_shape=(block, block, block),
        in_specs=[vmem] * 3,
        out_specs=(vmem,) * 3,
        name="results",
    )(next_input, received, input_grad)
    return (next_input[None], received[None], input_grad[None])


def solution(mesh):
    return jax.shard_map(
        functools.partial(per_device, mesh.shape["tensor"], mesh.shape["section"]),
        mesh=mesh,
        in_specs=(
            P("section", "dp", "tensor"),
            P("section", None, "dp", "tensor"),
            P("section"),
            P("section", "dp", "tensor"),
            P("section", "tensor"),
            P("section", None, "tensor"),
            P("section", "tensor", None),
            P("section", "tensor", None),
        ),
        out_specs=(
            P("section", "dp", "tensor"),
            P("section", "dp", "tensor"),
            P("section", "dp", "tensor"),
        ),
        check_vma=False,
    )
```

```python
import functools

import jax
import jax.numpy as jnp
import numpy as np
from jax import lax
from jax.experimental import pallas as pl
from jax.experimental.pallas import tpu as pltpu
from jax.sharding import PartitionSpec as P

HEADS = 32
KVH = 4
HD = 128
PAIR = 2
TILE = 256
SUMROWS = 8
PIECES = 2

norm_eps = 1e-05
f32 = jnp.float32
bf16 = jnp.bfloat16


def rope_constants(tokens):
    half = HD // 2
    inverse = np.float32(10000.0) ** (
        np.float32(-2.0) * np.arange(half, dtype=np.float32) / np.float32(HD)
    )
    angles = np.arange(tokens, dtype=np.float32)[:, None] * inverse[None, :].astype(np.float32)
    cos, sin = np.cos(angles), np.sin(angles)
    return (
        np.concatenate([cos, cos], axis=1).astype(np.float32),
        np.concatenate([-sin, sin], axis=1).astype(np.float32),
    )


def flipped(index, bits):
    place = 1
    while place <= bits:
        if bits & place:
            bit = lax.rem(lax.div(index, place), 2)
            index = index + place * (1 - 2 * bit)
        place *= 2
    return index


def dot_nn(a, b):
    return jnp.dot(a, b, preferred_element_type=f32)


def dot_nt(a, b):
    return lax.dot_general(a, b, (((1,), (1,)), ((), ())), preferred_element_type=f32)


def dot_tn(a, b):
    return lax.dot_general(a, b, (((0,), (0,)), ((), ())), preferred_element_type=f32)


def layer_kernel(
    ways,
    sections,
    slot_ref,
    x_ref,
    stash_ref,
    cot_ref,
    gain_ref,
    cos_ref,
    sin_ref,
    qw_hbm,
    kvw_hbm,
    ow_hbm,
    next_ref,
    travel_ref,
    igrad_ref,
    qw,
    kvw,
    ow,
    cg,
    fn,
    bn,
    back,
    c_acc,
    f_acc,
    b_acc,
    qf,
    qb,
    go,
    att,
    gqb,
    kvf_p,
    kvf_r,
    kvb_p,
    kvb_r,
    out_p,
    out_s,
    out_r,
    gq_p,
    gq_s,
    gq_r,
    gk_r,
    gk_acc,
    gk_full,
    trav,
    lo,
    gl,
    f_sum,
    b_sum,
    t_sum,
    m_sum,
    wsem,
    ssem,
    rsem,
):
    tokens, width = x_ref.shape
    heads_here = qw.shape[1] // HD
    model = width * ways
    half = tokens // 2
    upper, lower = pl.ds(0, half), pl.ds(half, half)
    me = lax.axis_index("tensor")
    sec = lax.axis_index("section")
    early = sec < sections // 2
    has_prev = sec > 0
    has_next = sec < sections - 1
    mirror = sections - 1 - sec
    prev = jnp.maximum(sec - 1, 0)
    nxt = jnp.minimum(sec + 1, sections - 1)
    peers = [flipped(me, k) for k in range(ways)]
    rows_of = [pl.ds(pl.multiple_of(p * width, width), width) for p in peers]
    relay = ways == 4
    per_group = ways // KVH
    groups = [lax.div(p, per_group) for p in peers]
    pieces = PIECES if width % (PIECES * TILE) == 0 else 1
    piece_width = width // pieces
    piece_cols = [pl.ds(p * piece_width, piece_width) for p in range(pieces)]

    load_kvw, load_qw, load_ow = [
        pltpu.make_async_copy(a, b, wsem.at[i])
        for i, (a, b) in enumerate(((kvw_hbm, kvw), (qw_hbm, qw), (ow_hbm, ow)))
    ]
    for load in (load_kvw, load_qw, load_ow):
        load.start()

    used = []
    pending = []

    def send(src, dst, axis, peer, start=True):
        i = len(used)
        used.append(i)
        copy = pltpu.make_async_remote_copy(
            src_ref=src,
            dst_ref=dst,
            send_sem=ssem.at[i],
            recv_sem=rsem.at[i],
            device_id=axis if peer is None else {axis: peer},
            device_id_type=pl.DeviceIdType.MESH,
        )
        if start:
            copy.start()
            pending.append(copy)
        return copy

    def to_peer(k, src, dst):
        return send(src, dst, "tensor", peers[k])

    barrier = pltpu.get_barrier_semaphore()

    def greet(axis, peer):
        pl.semaphore_signal(
            barrier, inc=1, device_id={axis: peer}, device_id_type=pl.DeviceIdType.MESH
        )

    for k in range(1, ways):
        greet("tensor", peers[k])
    for k in range(ways):
        pl.semaphore_signal(
            barrier,
            inc=1,
            device_id={"section": mirror, "tensor": peers[k]},
            device_id_type=pl.DeviceIdType.MESH,
        )

    @pl.when(has_prev)
    def _():
        greet("section", prev)

    @pl.when(has_next)
    def _():
        greet("section", nxt)

    @pl.when(early)
    def _():
        trav[...] = x_ref[...]

    @pl.when(jnp.logical_not(early))
    def _():
        trav[...] = stash_ref[slot_ref[0]]

    cg[0] = cot_ref[...]

    eye = lax.broadcasted_iota(jnp.int32, (tokens, tokens), 0) == lax.broadcasted_iota(
        jnp.int32, (tokens, tokens), 1
    )
    step = 32

    def squares(rows_ref):
        sums = []
        for r in range(0, tokens, step):
            v = rows_ref[r : r + step, :].astype(f32)
            sums.append(jnp.sum(v * v, axis=-1, keepdims=True))
        return jnp.concatenate(sums, axis=0)

    def sum_put(column, buf):
        as_row = jnp.sum(jnp.where(eye, column, 0.0), axis=0, keepdims=True)
        buf[0] = jnp.broadcast_to(as_row, (SUMROWS, tokens))

    def sum_send(buf):
        return [to_peer(k, buf.at[0], buf.at[k]) for k in range(1, ways)]

    def sum_total(copies, buf):
        finish(copies)
        total = buf[0, 0:1, :]
        for k in range(1, ways):
            total = total + buf[k, 0:1, :]
        return jnp.sum(jnp.where(eye, total, 0.0), axis=1, keepdims=True)

    def normalize(rows_ref, out, factor, first, last):
        for r in range(first, last, step):
            v = rows_ref[r : r + step, :].astype(f32)
            out[0, r : r + step, :] = (v * factor[r : r + step] * gain_ref[...]).astype(bf16)

    sum_put(squares(x_ref), f_sum)
    sum_put(squares(trav), t_sum)
    pl.semaphore_wait(barrier, 2 * ways - 1 + jnp.minimum(sec, 1) + jnp.minimum(sections - 1 - sec, 1))

    def gather_first(buf):
        if relay:
            return [
                to_peer(1, buf.at[0, upper], buf.at[1, upper]),
                to_peer(2, buf.at[0, lower], buf.at[2, lower]),
            ]
        return [to_peer(k, buf.at[0], buf.at[k]) for k in range(1, ways)]

    def gather_second(buf):
        if relay:
            return [
                to_peer(1, buf.at[0, lower], buf.at[1, lower]),
                to_peer(2, buf.at[0, upper], buf.at[2, upper]),
            ]
        return []

    def gather_pass_on(buf, copies):
        if not relay:
            finish(copies)
            return []
        copies[0].wait_recv()
        first = to_peer(2, buf.at[1, upper], buf.at[3, upper])
        copies[1].wait_recv()
        second = to_peer(1, buf.at[2, lower], buf.at[3, lower])
        return [first, second]

    def finish(copies):
        for copy in copies:
            copy.wait_recv()

    order = (3, 1, 2, 0) if relay else tuple(range(1, ways)) + (0,)

    def reduce_send(k, stage, land, cols):
        if k == 0:
            return []
        if not relay:
            return [to_peer(k, stage.at[k, :, cols], land.at[k, :, cols])]
        if k == 3:
            return [
                to_peer(1, stage.at[3, upper, cols], land.at[2, upper, cols]),
                to_peer(2, stage.at[3, lower, cols], land.at[1, lower, cols]),
            ]
        if k == 1:
            return [to_peer(1, stage.at[1, upper, cols], land.at[0, upper, cols])]
        return [to_peer(2, stage.at[2, lower, cols], land.at[0, lower, cols])]

    def reduce_pass_on(copies, part, stage, land, cols):
        if not relay:
            return copies
        copies[0].wait_recv()
        summed = part[2, upper, cols] + land[2, upper, cols].astype(f32)
        stage[2, upper, cols] = summed.astype(stage.dtype)
        first = to_peer(2, stage.at[2, upper, cols], land.at[3, upper, cols])
        copies[1].wait_recv()
        summed = part[1, lower, cols] + land[1, lower, cols].astype(f32)
        stage[1, lower, cols] = summed.astype(stage.dtype)
        second = to_peer(1, stage.at[1, lower, cols], land.at[3, lower, cols])
        return copies[2:] + [first, second]

    def reduced(part, land, rows, cols):
        total = part[0, rows, cols]
        for k in (0, 3) if relay else range(1, ways):
            total = total + land[k, rows, cols].astype(f32)
        return total

    def tile_loop(count, body):
        lax.fori_loop(0, count, body, 0, unroll=2 if count % 2 == 0 else 1)

    kv_cols = pl.ds(0, 2 * HD)
    all_cols = pl.ds(0, width)
    everything = pl.ds(0, tokens)

    def kv_terms(normed, part, land):
        copies = []
        for k in order:
            key_cols = pl.ds(pl.multiple_of(groups[k] * HD, HD), HD)
            value_cols = pl.ds(pl.multiple_of((KVH + groups[k]) * HD, HD), HD)
            part[k, :, 0:HD] = dot_nn(normed[0], kvw[:, key_cols])
            part[k, :, HD : 2 * HD] = dot_nn(normed[0], kvw[:, value_cols])
            copies += reduce_send(k, part, land, kv_cols)
        return copies

    def rotate(u):
        return u * cos_ref[...] + pltpu.roll(u, HD // 2, 1) * sin_ref[...]

    def unrotate(u):
        return u * cos_ref[...] - pltpu.roll(u, HD // 2, 1) * sin_ref[...]

    per_tile = TILE // HD
    scale = HD ** (-0.5)

    def accumulate(ks, buf, weight_tile, acc, out=None, finished=None):
        def body(n, carry):
            cols = pl.ds(pl.multiple_of(n * TILE, TILE), TILE)
            total = weight_tile(buf, ks[0], cols)
            for k in ks[1:]:
                total = total + weight_tile(buf, k, cols)
            if ks[0] != 0:
                total = total + acc[:, cols]
            acc[:, cols] = total
            if out is not None:
                for j in range(per_tile):
                    head = total[:, j * HD : (j + 1) * HD]
                    out[n * per_tile + j] = finished(head).astype(bf16)
            return carry

        tile_loop(heads_here // per_tile, body)

    def query_block(buf, k, cols):
        return dot_nn(buf[k], qw[rows_of[k], cols])

    def cot_block(buf, k, rows):
        return dot_nt(buf[k], ow[rows, rows_of[k]])

    def turned_query(head):
        return rotate(head) * scale

    def plain(head):
        return head

    near = [1, 2] if relay else list(range(1, ways // 2))
    far = [3] if relay else list(range(ways // 2, ways))

    def key_value(part, land):
        key_wide = reduced(part, land, everything, pl.ds(0, HD))
        value_wide = reduced(part, land, everything, pl.ds(HD, HD))
        return rotate(key_wide).astype(bf16), value_wide.astype(bf16), key_wide, value_wide

    span = PAIR * tokens
    position = lax.rem(lax.broadcasted_iota(jnp.int32, (span, tokens), 0), tokens)
    seen = position >= lax.broadcasted_iota(jnp.int32, (span, tokens), 1)

    def probabilities(q, key):
        scores = jnp.where(seen, dot_nt(q, key), -1e30)
        shifted = jnp.exp(scores - jnp.max(scores, axis=-1, keepdims=True))
        return shifted * (1.0 / jnp.sum(shifted, axis=-1, keepdims=True))

    def project(source, weight_tile, part, stage, k, first, count):
        def body(n, carry):
            n = first + n
            cols = pl.ds(pl.multiple_of(n * TILE, TILE), TILE)
            value = weight_tile(source, k, n)
            if not (relay and k == 3):
                part[k, :, cols] = value
            if k:
                stage[k, :, cols] = value.astype(bf16)
            return carry

        tile_loop(count, body)

    def out_tile(source, k, n):
        cols = pl.ds(pl.multiple_of(peers[k] * width + n * TILE, TILE), TILE)
        return dot_nn(source[...], ow[:, cols])

    def query_tile(source, k, n):
        rows = pl.ds(pl.multiple_of(peers[k] * width + n * TILE, TILE), TILE)
        return dot_nt(source[...], qw[rows, :])

    travel_copies = [
        send(trav.at[rows], travel_ref.at[rows], "section", mirror) for rows in (upper, lower)
    ]
    f_sums = sum_send(f_sum)
    b_sums = [
        send(t_sum.at[0], b_sum.at[k], {"section": mirror, "tensor": peers[k]}, None)
        for k in range(ways)
    ]
    c_first = gather_first(cg)
    f_total = sum_total(f_sums, f_sum)
    normalize(x_ref, fn, lax.rsqrt(f_total / model + norm_eps), 0, tokens)
    x_first = gather_first(fn)
    x_second = gather_second(fn)
    load_kvw.wait()
    kvf = kv_terms(fn, kvf_p, kvf_r)
    load_qw.wait()
    accumulate([0], fn, query_block, f_acc)
    x_far = gather_pass_on(fn, x_first)
    c_far = gather_pass_on(cg, c_first)
    c_second = gather_second(cg)
    kvf = reduce_pass_on(kvf, kvf_p, kvf_p, kvf_r, kv_cols)
    b_total = jnp.where(early, sum_total(b_sums, b_sum), f_total)
    factor = lax.rsqrt(b_total / model + norm_eps)

    def take_back(copy, rows, first):
        copy.wait_recv()

        @pl.when(early)
        def _():
            back[rows, :] = travel_ref[rows, :]

        @pl.when(jnp.logical_not(early))
        def _():
            back[rows, :] = x_ref[rows, :]

        normalize(back, bn, factor, first, first + half)

    take_back(travel_copies[0], upper, 0)
    if relay:
        b_first = [to_peer(1, bn.at[0, upper], bn.at[1, upper])]
        b_second = [to_peer(2, bn.at[0, upper], bn.at[2, upper])]
    finish(x_second)
    accumulate(near, fn, query_block, f_acc)
    take_back(travel_copies[1], lower, half)
    if relay:
        b_first.append(to_peer(2, bn.at[0, lower], bn.at[2, lower]))
        b_second.append(to_peer(1, bn.at[0, lower], bn.at[1, lower]))
    else:
        b_first = gather_first(bn)
        b_second = []
    kvb = kv_terms(bn, kvb_p, kvb_r)
    finish(x_far)
    accumulate(far, fn, query_block, f_acc, qf, turned_query)
    finish(kvf)
    key, value, _, _ = key_value(kvf_p, kvf_r)
    for i in range(heads_here // PAIR):
        q = qf[PAIR * i : PAIR * (i + 1)].reshape(span, HD)
        weights = probabilities(q, key).astype(bf16)
        result = dot_nn(weights, value).astype(bf16)
        for j in range(PAIR):
            head = PAIR * i + j
            att[:, head * HD : (head + 1) * HD] = result[j * tokens : (j + 1) * tokens]

    b_far = gather_pass_on(bn, b_first)
    load_ow.wait()
    for k in order:
        project(att, out_tile, out_p, out_s, k, 0, width // TILE)
    kvb = reduce_pass_on(kvb, kvb_p, kvb_p, kvb_r, kv_cols)
    finish(c_second)
    finish(c_far)
    accumulate(list(range(ways)), cg, cot_block, c_acc, go, plain)
    finish(b_second)
    accumulate([0] + near, bn, query_block, b_acc)
    finish(b_far)
    outs = []
    for k in order:
        outs += reduce_send(k, out_s, out_r, all_cols)
    accumulate(far, bn, query_block, b_acc, qb, turned_query)

    finish(kvb)
    key, value, key_wide, value_wide = key_value(kvb_p, kvb_r)
    grad_key = jnp.zeros((tokens, HD), f32)
    grad_value = jnp.zeros((tokens, HD), f32)
    mixed = jnp.zeros((tokens, HD), f32)
    for i in range(heads_here // PAIR):
        if i == heads_here // PAIR // 2:
            outs = reduce_pass_on(outs, out_p, out_s, out_r, all_cols)
        q = qb[PAIR * i : PAIR * (i + 1)].reshape(span, HD)
        g = go[PAIR * i : PAIR * (i + 1)].reshape(span, HD)
        probs = probabilities(q, key)
        grad_probs = dot_nt(g, value)
        delta = jnp.sum(probs * grad_probs, axis=-1, keepdims=True)
        grad_scores = (probs * (grad_probs - delta)).astype(bf16)
        grad_q = dot_nn(grad_scores, key)
        for j in range(PAIR):
            head = PAIR * i + j
            turned = (unrotate(grad_q[j * tokens : (j + 1) * tokens]) * scale).astype(bf16)
            gqb[:, head * HD : (head + 1) * HD] = turned
            mixed = mixed + turned.astype(f32) * b_acc[:, head * HD : (head + 1) * HD]
        grad_key = grad_key + dot_tn(grad_scores, q)
        grad_value = grad_value + dot_tn(probs.astype(bf16), g)
    grad_key = unrotate(grad_key).astype(gk_r.dtype)
    grad_value = grad_value.astype(gk_r.dtype)
    gk_r[0, :, 0:HD] = grad_key
    gk_r[0, :, HD : 2 * HD] = grad_value
    gk_copies = [to_peer(k, gk_r.at[0], gk_r.at[k]) for k in range(1, ways)]
    mixed = mixed + grad_key.astype(f32) * key_wide + grad_value.astype(f32) * value_wide
    sum_put(jnp.sum(mixed, axis=-1, keepdims=True), m_sum)
    m_sums = sum_send(m_sum)
    grads = []
    piece_tiles = piece_width // TILE
    for p in range(pieces):
        grads.append([])
        for k in order:
            project(gqb, query_tile, gq_p, gq_s, k, p * piece_tiles, piece_tiles)
            grads[p] += reduce_send(k, gq_s, gq_r, piece_cols[p])

    next_copies = []
    grad_copies = []
    row_chunks = (upper, lower)

    finish(outs)
    for rows in row_chunks:
        total = reduced(out_p, out_r, rows, all_cols)
        lo[rows, :] = (x_ref[rows, :].astype(f32) + total).astype(bf16)
        copy = send(lo.at[rows], next_ref.at[rows], "section", nxt, start=False)
        pl.when(has_next)(copy.start)
        next_copies.append(copy)
    for p in range(pieces):
        grads[p] = reduce_pass_on(grads[p], gq_p, gq_s, gq_r, piece_cols[p])

    finish(gk_copies)
    if per_group == 1:
        for k in range(ways):
            key_cols = pl.ds(pl.multiple_of(groups[k] * HD, HD), HD)
            value_cols = pl.ds(pl.multiple_of((KVH + groups[k]) * HD, HD), HD)
            gk_full[:, key_cols] = gk_r[k, :, 0:HD]
            gk_full[:, value_cols] = gk_r[k, :, HD : 2 * HD]
    else:
        gk_acc[...] = jnp.zeros_like(gk_acc)
        for k in range(ways):
            key_cols = pl.ds(pl.multiple_of(groups[k] * HD, HD), HD)
            value_cols = pl.ds(pl.multiple_of((KVH + groups[k]) * HD, HD), HD)
            gk_acc[:, key_cols] += gk_r[k, :, 0:HD].astype(f32)
            gk_acc[:, value_cols] += gk_r[k, :, HD : 2 * HD].astype(f32)
        gk_full[...] = gk_acc[...].astype(bf16)
    for n in range(width // TILE):
        cols = pl.ds(n * TILE, TILE)
        gq_p[0, :, cols] += dot_nt(gk_full[...], kvw[cols, :])
    square_mean = factor * factor * (sum_total(m_sums, m_sum) / model)

    for p in range(pieces):
        finish(grads[p])
        cols = piece_cols[p]
        for c, rows in enumerate(row_chunks):
            here = slice(c * half, (c + 1) * half)
            g = reduced(gq_p, gq_r, rows, cols) * gain_ref[:, cols]
            b = back[rows, cols].astype(f32)
            grad_rows = factor[here] * g - b * square_mean[here]
            gl[rows, cols] = (cot_ref[rows, cols].astype(f32) + grad_rows).astype(bf16)
            copy = send(gl.at[rows, cols], igrad_ref.at[rows, cols], "section", prev, start=False)
            pl.when(has_prev)(copy.start)
            grad_copies.append(copy)

    @pl.when(jnp.logical_not(has_prev))
    def _():
        next_ref[...] = jnp.zeros_like(next_ref)

    @pl.when(jnp.logical_not(has_next))
    def _():
        igrad_ref[...] = jnp.zeros_like(igrad_ref)

    for copy in pending:
        copy.wait_send()

    @pl.when(has_next)
    def _():
        for copy in next_copies:
            copy.wait_send()
        for copy in grad_copies:
            copy.wait_recv()

    @pl.when(has_prev)
    def _():
        for copy in next_copies:
            copy.wait_recv()
        for copy in grad_copies:
            copy.wait_send()


def hand_on(a, b, c, a_out, b_out, c_out):
    a_out[...] = a[...]
    b_out[...] = b[...]
    c_out[...] = c[...]


def copies_needed(ways):
    if ways == 4:
        return 2 + 6 + 4 + 3 * 6 + 2 * 6 + 6 + PIECES * 6 + 3 + 2 + 2 * PIECES
    return 3 + (ways - 1) * (3 + 3 + 2 + 2 * PIECES + 1) + 4 * PIECES


def per_device(
    ways,
    sections,
    section_input,
    stash_pool,
    reload_slot,
    cotangent,
    norm_gain,
    query_weight,
    kv_weight,
    out_weight,
):
    _, tokens, width = section_input.shape
    model = width * ways
    local = query_weight.shape[2]
    heads_here = local // HD
    cos_table, sin_table = rope_constants(tokens)
    grad_kv_type = bf16 if ways == KVH else f32
    copies = copies_needed(ways)
    vmem = pl.BlockSpec(memory_space=pltpu.VMEM)
    block = jax.ShapeDtypeStruct((tokens, width), bf16)
    gathered = pltpu.VMEM((ways, tokens, width), bf16)
    wide = pltpu.VMEM((ways, tokens, width), f32)
    kv_block = pltpu.VMEM((ways, tokens, 2 * HD), f32)
    head_block = pltpu.VMEM((heads_here, tokens, HD), bf16)
    flat = pltpu.VMEM((tokens, local), bf16)
    sums = pltpu.VMEM((ways, SUMROWS, tokens), f32)
    local_wide = pltpu.VMEM((tokens, local), f32)
    flat_block = pltpu.VMEM((tokens, width), bf16)
    scratch = [
        pltpu.VMEM((model, local), bf16),
        pltpu.VMEM((width, 2 * KVH * HD), bf16),
        pltpu.VMEM((local, model), bf16),
        gathered,
        gathered,
        gathered,
        flat_block,
        local_wide,
        local_wide,
        local_wide,
        head_block,
        head_block,
        head_block,
        flat,
        flat,
        kv_block,
        kv_block,
        kv_block,
        kv_block,
        wide,
        gathered,
        gathered,
        wide,
        gathered,
        gathered,
        pltpu.VMEM((ways, tokens, 2 * HD), grad_kv_type),
        pltpu.VMEM((tokens, 2 * KVH * HD), f32),
        pltpu.VMEM((tokens, 2 * KVH * HD), bf16),
        flat_block,
        flat_block,
        flat_block,
        sums,
        sums,
        pltpu.VMEM((1, SUMROWS, tokens), f32),
        sums,
        pltpu.SemaphoreType.DMA((3,)),
        pltpu.SemaphoreType.DMA((copies,)),
        pltpu.SemaphoreType.DMA((copies,)),
    ]
    macs = 5 * tokens * model * local + 3 * tokens * width * 2 * KVH * HD
    next_input, received, input_grad = pl.pallas_call(
        functools.partial(layer_kernel, ways, sections),
        out_shape=(block, block, block),
        in_specs=[pl.BlockSpec(memory_space=pltpu.SMEM)]
        + [vmem] * 6
        + [pl.BlockSpec(memory_space=pl.ANY)] * 3,
        out_specs=(vmem, vmem, vmem),
        scratch_shapes=scratch,
        cost_estimate=pl.CostEstimate(
            flops=2 * macs,
            bytes_accessed=2 * (2 * model * local + width * 2 * KVH * HD + 8 * tokens * width),
            transcendentals=2 * heads_here * tokens * tokens,
        ),
        compiler_params=pltpu.CompilerParams(
            collective_id=0, has_side_effects=True, vmem_limit_bytes=56 * 1024 * 1024
        ),
        name="attention_layer",
    )(
        reload_slot,
        section_input[0],
        stash_pool[0],
        cotangent[0],
        norm_gain,
        jnp.asarray(cos_table),
        jnp.asarray(sin_table),
        query_weight[0],
        kv_weight[0],
        out_weight[0],
    )
    next_input, received, input_grad = pl.pallas_call(
        hand_on,
        out_shape=(block, block, block),
        in_specs=[vmem] * 3,
        out_specs=(vmem,) * 3,
        name="results",
    )(next_input, received, input_grad)
    return (next_input[None], received[None], input_grad[None])


def solution(mesh):
    return jax.shard_map(
        functools.partial(per_device, mesh.shape["tensor"], mesh.shape["section"]),
        mesh=mesh,
        in_specs=(
            P("section", "dp", "tensor"),
            P("section", None, "dp", "tensor"),
            P("section"),
            P("section", "dp", "tensor"),
            P("section", "tensor"),
            P("section", None, "tensor"),
            P("section", "tensor", None),
            P("section", "tensor", None),
        ),
        out_specs=(
            P("section", "dp", "tensor"),
            P("section", "dp", "tensor"),
            P("section", "dp", "tensor"),
        ),
        check_vma=False,
    )
```
